32 devices in a mesh: seq: 8 (over z, x), head: 4 (over y, core).
Axes of the slice: x: 2, y: 2, z: 4, core: 2. Of those that a mesh axis runs over, the one named last changes fastest.
Arguments:
- queries: bfloat16 [2048, 8192], P('seq', 'head'), may hold values from -6 to 6
- key_rows: bfloat16 [2048, 8192], P('seq', 'head'), may hold values from -6 to 6
- value_rows: bfloat16 [2048, 8192], P('seq', 'head'), may hold values from -160 to 160
- log_decay: float32 [2048, 64], P('seq', 'head'), may hold values from -0.5 to 0, as said below
- gate_input: bfloat16 [2048, 8192], P('seq', 'head'), may hold values from -12 to 12
- out_gain: float32 [8192], P('head'), may hold values from 0.1 to 1.9
- prior_state: float32 [64, 128, 128], P('head'), may hold values from -192 to 192
- out_grad: bfloat16 [2048, 8192], P('seq', 'head'), may hold values from -6 to 6
Outputs:
- attended: bfloat16 [2048, 8192], P('seq', 'head')
- grad_query: bfloat16 [2048, 8192], P('seq', 'head')
- grad_key: bfloat16 [2048, 8192], P('seq', 'head')
- grad_value: bfloat16 [2048, 8192], P('seq', 'head')
- grad_gate: bfloat16 [2048, 8192], P('seq', 'head')
The draws below stay inside these ranges and needn't reach their ends.
Inputs may be any that keep to these rules, and one draw needn't show every extreme that they name: `log_decay`: every entry is negative; at each token a head's state is multiplied by exp(entry).
All inputs are finite; a program needn't handle non-finite values.
Results may differ from the reference program's by a relative error of at most 0.012.
Values sent between devices are 32-bit elements; how exact they have to be, the bound alone decides.
A program may use at most 64 MiB of HBM per device.

```python
import math
import jax
import jax.numpy as jnp
from jax import lax

HEAD_TOTAL = 64
HD = 128
BLK = 256
D = 8192
WINDOW_TOKENS = 2048


def draw_log_decay(key, part):
    pick_key, slow_key, fast_key, rough_key, location_key, falloff_key = jax.random.split(key, 6)
    pick_draw = jax.random.randint(pick_key, (HEAD_TOTAL,), 0, 10)
    is_slow = pick_draw < 5
    slow_rate = jnp.exp(jax.random.uniform(slow_key, (HEAD_TOTAL,), jnp.float32, math.log(4e-06), math.log(4e-05)))
    fast_rate = jnp.exp(jax.random.uniform(fast_key, (HEAD_TOTAL,), jnp.float32, math.log(0.02), math.log(0.033)))
    decay_speed = jnp.where(is_slow, slow_rate, fast_rate)
    jaggedness = jax.random.uniform(rough_key, (WINDOW_TOKENS, HEAD_TOTAL), jnp.float32, 0.5, 1.5)
    spike_position = jax.random.randint(location_key, (3,), 0, WINDOW_TOKENS)
    spike_row = jnp.any(jnp.arange(WINDOW_TOKENS)[:, None] == spike_position[None, :], axis=1)
    spike_falloff = jax.random.uniform(falloff_key, (WINDOW_TOKENS, HEAD_TOTAL), jnp.float32, 0.22, 0.5)
    return jnp.where(spike_row[:, None], -spike_falloff, -decay_speed[None, :] * jaggedness).astype(jnp.float32)


def draw_value_rows(key, part):
    ramp_key = jax.random.fold_in(key, 0)
    base_key = jax.random.fold_in(key, 1)
    row_key = jax.random.fold_in(key, 3)
    head_place = (jnp.arange(D) // HD).astype(jnp.float32) / (HEAD_TOTAL - 1)
    column_scale = jnp.exp(math.log(3.0) * head_place + jax.random.uniform(ramp_key, (D,), jnp.float32, 0.0, math.log(10.0 / 3.0)))
    base_draw = jnp.clip(jax.random.normal(base_key, (WINDOW_TOKENS, D), jnp.float32), -4.0, 4.0)
    row_scale = jnp.exp(jax.random.uniform(row_key, (WINDOW_TOKENS, 1), jnp.float32, 0.0, math.log(4.0)))
    return (base_draw * column_scale[None, :] * row_scale).astype(jnp.bfloat16)


def shard_levels(rng, extent, cuts, low, high):
    loudness = 1.0
    for dim, shards_of in cuts:
        draws = jax.random.uniform(jax.random.fold_in(jax.random.fold_in(rng, 6), dim), (shards_of,), jnp.float32, low / len(cuts), high / len(cuts))
        loudness = loudness * jnp.repeat(jnp.exp(draws), extent[dim] // shards_of).reshape((-1,) + (1,) * (len(extent) - 1 - dim))
    return loudness


def scatter_about(stream_key, extent, scale, limit, cuts=(), dtype=jnp.bfloat16):
    array = jax.random.normal(stream_key, extent, jnp.float32) * scale
    if len(cuts) > 0:
        array = shard_levels(stream_key, extent, cuts, -0.22, 0.18) * array
    return jnp.clip(array, min=-limit, max=limit).astype(dtype)


def setup_inputs(seed: int = 0) -> dict:
    splits = jax.random.split(jax.random.key(seed), 9)
    return {
        "queries": scatter_about(splits[0], (WINDOW_TOKENS, D), 1.0, 6.0, ((0, 8), (1, 4))),
        "key_rows": scatter_about(splits[1], (WINDOW_TOKENS, D), 1.0, 6.0, ((0, 8), (1, 4))),
        "value_rows": draw_value_rows(jax.random.fold_in(splits[8], 71), 0),
        "log_decay": draw_log_decay(jax.random.fold_in(splits[8], 71), 0),
        "gate_input": scatter_about(splits[4], (WINDOW_TOKENS, D), 2.0, 12.0, ((0, 8), (1, 4))),
        "out_gain": jnp.clip(1.0 + 0.18 * jax.random.normal(splits[5], (D,), jnp.float32), 0.1, 1.9),
        "prior_state": scatter_about(splits[6], (HEAD_TOTAL, HD, HD), 32.0, 192.0, ((0, 4),), jnp.float32),
        "out_grad": scatter_about(splits[7], (WINDOW_TOKENS, D), 1.0, 6.0, ((0, 8), (1, 4))),
    }


epsilon = 1e-06
highest = lax.Precision.HIGHEST

def decay_tables(decay_block):
    running = jnp.cumsum(decay_block, axis=0)
    closing = running[-1]
    spread = running.T[:, :, None] - running.T[:, None, :]
    causal = jnp.arange(decay_block.shape[0])[:, None] >= jnp.arange(decay_block.shape[0])[None, :]
    weights = jnp.where(causal[None], jnp.exp(jnp.minimum(spread, 0.0)), 0.0)
    return (running, closing, weights)

def mixing_of(query_wide, key_wide, weights):
    scores = jnp.einsum('the,she->hts', query_wide, key_wide, precision=highest)
    mixing = (scores * weights).astype(jnp.bfloat16)
    return lax.optimization_barrier(mixing).astype(jnp.float32)

def forward_step(carried, inputs):
    query_block, key_block, value_block, decay_block = inputs
    running, closing, weights = decay_tables(decay_block)
    query_wide = query_block.astype(jnp.float32)
    key_wide = key_block.astype(jnp.float32)
    value_wide = value_block.astype(jnp.float32)
    mixing = mixing_of(query_wide, key_wide, weights)
    within = jnp.einsum('hts,she->the', mixing, value_wide, precision=highest)
    across = jnp.exp(running)[:, :, None] * jnp.einsum('the,hef->thf', query_wide, carried, precision=highest)
    remain = jnp.exp(closing[None, :] - running)
    updated = jnp.exp(closing)[:, None, None] * carried + jnp.einsum('she,shf->hef', key_wide * remain[:, :, None], value_wide, precision=highest)
    return (updated, (within + across, carried))

def backward_step(returned, inputs):
    query_block, key_block, value_block, grad_rows, decay_block, opening = inputs
    running, closing, weights = decay_tables(decay_block)
    query_wide = query_block.astype(jnp.float32)
    key_wide = key_block.astype(jnp.float32)
    value_wide = value_block.astype(jnp.float32)
    grad_wide = grad_rows.astype(jnp.float32)
    mixing = mixing_of(query_wide, key_wide, weights)
    grad_scores = jnp.einsum('thf,shf->hts', grad_wide, value_wide, precision=highest)
    grad_mixing = lax.optimization_barrier((grad_scores * weights).astype(jnp.bfloat16)).astype(jnp.float32)
    grad_q = jnp.einsum('hts,she->the', grad_mixing, key_wide, precision=highest) + jnp.exp(running)[:, :, None] * jnp.einsum('thf,hef->the', grad_wide, opening, precision=highest)
    remain = jnp.exp(closing[None, :] - running)[:, :, None]
    grad_k = jnp.einsum('hts,the->she', grad_mixing, query_wide, precision=highest) + remain * jnp.einsum('shf,hef->she', value_wide, returned, precision=highest)
    grad_v = jnp.einsum('hts,thf->shf', mixing, grad_wide, precision=highest) + remain * jnp.einsum('she,hef->shf', key_wide, returned, precision=highest)
    summed = jnp.einsum('the,thf->hef', query_wide * jnp.exp(running)[:, :, None], grad_wide, precision=highest)
    updated = summed + jnp.exp(closing)[:, None, None] * returned
    return (updated, (grad_q, grad_k, grad_v))

def reference(queries, key_rows, value_rows, log_decay, gate_input, out_gain, prior_state, out_grad):
    blocks = WINDOW_TOKENS // BLK
    block_shape = (blocks, BLK, HEAD_TOTAL, HD)
    query_all = queries.reshape(block_shape)
    key_all = key_rows.reshape(block_shape)
    value_all = value_rows.reshape(block_shape)
    decay_all = log_decay.reshape(blocks, BLK, HEAD_TOTAL)
    final_state, (context_parts, openings) = lax.scan(forward_step, prior_state.astype(jnp.float32), (query_all, key_all, value_all, decay_all))
    merged = context_parts.reshape(WINDOW_TOKENS, D)
    inverse = lax.rsqrt(lax.optimization_barrier(jnp.sum(merged * merged, axis=1)) / D + epsilon)
    normed = merged * inverse[:, None]
    opened = jax.nn.sigmoid(gate_input.astype(jnp.float32))
    attended = (normed * out_gain * opened).astype(jnp.bfloat16)
    grad_wide = out_grad.astype(jnp.float32)
    grad_gate = (grad_wide * normed * out_gain * opened * (1.0 - opened)).astype(jnp.bfloat16)
    grad_norm = grad_wide * out_gain * opened
    row_dot = lax.optimization_barrier(jnp.sum(merged * grad_norm, axis=1))
    grad_merged = inverse[:, None] * grad_norm - merged * (inverse * inverse * inverse * row_dot / D)[:, None]
    grad_context = grad_merged.astype(jnp.bfloat16)
    grad_all = grad_context.reshape(block_shape)
    zero_state = jnp.zeros((HEAD_TOTAL, HD, HD), jnp.float32)
    unused, (grad_q_parts, grad_k_parts, grad_v_parts) = lax.scan(backward_step, zero_state, (query_all, key_all, value_all, grad_all, decay_all, openings), reverse=True)
    grad_query = grad_q_parts.reshape(WINDOW_TOKENS, D).astype(jnp.bfloat16)
    grad_key = grad_k_parts.reshape(WINDOW_TOKENS, D).astype(jnp.bfloat16)
    grad_value = grad_v_parts.reshape(WINDOW_TOKENS, D).astype(jnp.bfloat16)
    return (attended, grad_query, grad_key, grad_value, grad_gate)
```

```python
import functools

import jax
import jax.numpy as jnp
from jax import lax
from jax.experimental import pallas as pl
from jax.experimental.pallas import tpu as pltpu
from jax.sharding import PartitionSpec as P

BLK = 256
D = 8192
HD = 128
epsilon = 1e-06
MESH = pl.DeviceIdType.MESH
F32 = jnp.float32
BF16 = jnp.bfloat16


def dot(a, b, ca, cb):
    return lax.dot_general(a, b, (((ca,), (cb,)), ((), ())), preferred_element_type=F32)


def kernel(
    n_seq, n_head, heads,
    q_hbm, k_hbm, v_hbm, ld_ref, gate_hbm, gain_ref, prior_hbm, og_hbm,
    att_hbm, gq_hbm, gk_hbm, gv_hbm, gg_hbm,
    q, k, v, gate, og, prior,
    att, gq, gk, gv, gg,
    run_col, run_row, dec, dec_x,
    own, cross, enter, part, pass_z, pass_x, used,
    own_b, cross_b, enter_b, part_b, pass_z_b, pass_x_b,
    wts, mix, ctx, gnorm, grad, gk_acc, gv_acc,
    sq_acc, rd_acc, sums, sums_in,
    in_sem, out_sem, dec_send, dec_recv, sum_send, sum_recv,
    s_send, s_recv, z_send, z_recv, x_send, x_recv,
    bs_send, bs_recv, bz_send, bz_recv, bx_send, bx_recv,
):
    half = heads // 2
    me = lax.axis_index("seq")
    row = lax.axis_index("head")
    pair, side = me // 2, me % 2
    last = n_seq // 2 - 1
    partner = me + 1 - 2 * side
    mine, theirs = side * half, (1 - side) * half

    barrier = pltpu.get_barrier_semaphore()

    def greet(**target):
        pl.semaphore_signal(barrier, inc=1, device_id=target, device_id_type=MESH)

    greet(seq=partner)
    for d in range(1, n_head):
        greet(head=lax.rem(row + d, n_head))

    @pl.when(pair > 0)
    def _():
        greet(seq=me - 2)

    @pl.when(pair < last)
    def _():
        greet(seq=me + 2)

    loads = [
        pltpu.make_async_copy(src, dst, in_sem.at[j])
        for j, (src, dst) in enumerate(
            [(k_hbm, k), (v_hbm, v), (q_hbm, q), (gate_hbm, gate), (og_hbm, og), (prior_hbm, prior)]
        )
    ]
    for load in loads:
        load.start()

    ti = lax.broadcasted_iota(jnp.int32, (BLK, BLK), 0)
    si = lax.broadcasted_iota(jnp.int32, (BLK, BLK), 1)
    causal = ti >= si
    low = jnp.where(causal, 1.0, 0.0).astype(F32)
    ld = ld_ref[...]
    col = lax.dot_general(
        low, ld, (((1,), (0,)), ((), ())), precision=lax.Precision.HIGHEST, preferred_element_type=F32
    )
    run_row[...] = lax.dot_general(
        ld, low, (((0,), (1,)), ((), ())), precision=lax.Precision.HIGHEST, preferred_element_type=F32
    )
    for h in range(heads):
        wide = jnp.broadcast_to(col[:, h : h + 1], (BLK, HD))
        run_col[h] = wide
        dec[h : h + 1, :] = jnp.exp(wide[BLK - 1 : BLK, :])

    def cols(h):
        return pl.ds(pl.multiple_of(h * HD, HD), HD)

    def send(src, dst, s, r, **target):
        return pltpu.make_async_remote_copy(
            src_ref=src, dst_ref=dst, send_sem=s, recv_sem=r, device_id=target, device_id_type=MESH
        )

    sum_copies = [
        send(sums, sums_in.at[d - 1], sum_send.at[d - 1], sum_recv.at[d - 1], head=lax.rem(row + d, n_head))
        for d in range(1, n_head)
    ]
    dec_copy = send(dec, dec_x, dec_send, dec_recv, seq=partner)

    def s_copy(i):
        return send(own.at[theirs + i], cross.at[i], s_send.at[i], s_recv.at[i], seq=partner)

    def z_copy(i):
        return send(pass_z.at[i], enter.at[i], z_send.at[i], z_recv.at[i], seq=me + 2)

    def x_copy(i):
        return send(pass_x.at[i], part.at[i], x_send.at[i], x_recv.at[i], seq=partner)

    def bs_copy(i):
        return send(own_b.at[theirs + i], cross_b.at[i], bs_send.at[i], bs_recv.at[i], seq=partner)

    def bz_copy(i):
        return send(pass_z_b.at[i], enter_b.at[i], bz_send.at[i], bz_recv.at[i], seq=me - 2)

    def bx_copy(i):
        return send(pass_x_b.at[i], part_b.at[i], bx_send.at[i], bx_recv.at[i], seq=partner)

    def remain_of(h):
        wide = run_col[h]
        return jnp.exp(wide[BLK - 1 : BLK, :] - wide)

    def summary(h):
        scaled = (k[:, cols(h)].astype(F32) * remain_of(h)).astype(BF16)
        own[h] = dot(scaled, v[:, cols(h)], 0, 0)

    loads[0].wait()
    loads[1].wait()
    pl.semaphore_wait(
        barrier, n_head + jnp.where(pair > 0, 1, 0) + jnp.where(pair < last, 1, 0)
    )
    dec_copy.start()

    @pl.loop(0, half)
    def _(i):
        summary(theirs + i)
        s_copy(i).start()

    for load in loads[2:]:
        load.wait()
    dec_copy.wait_recv()
    sq_acc[...] = jnp.zeros_like(sq_acc)
    rd_acc[...] = jnp.zeros_like(rd_acc)

    def within(h):
        spread = jnp.broadcast_to(run_col[h][:, :1], (BLK, BLK)) - run_row[pl.ds(h, 1), :]
        w = jnp.where(causal, jnp.exp(jnp.minimum(spread, 0.0)), 0.0)
        wts[h] = w
        m = (dot(q[:, cols(h)], k[:, cols(h)], 1, 1) * w).astype(BF16)
        mix[h] = m
        ctx[h] = dot(m, v[:, cols(h)], 1, 0)
        opened = jax.nn.sigmoid(gate[:, cols(h)].astype(F32))
        gnorm[h] = og[:, cols(h)].astype(F32) * gain_ref[:, cols(h)] * opened

    def finish(h, state):
        c = ctx[h] + jnp.exp(run_col[h]) * dot(q[:, cols(h)], state.astype(BF16), 1, 0)
        ctx[h] = c
        sq_acc[...] += c * c
        rd_acc[...] += c * gnorm[h]

    first = side == 0

    @pl.loop(0, half)
    def _(i):
        h = mine + i
        summary(h)
        within(h)
        within(theirs + i)

        @pl.when(pair == 0)
        def _():
            enter[i] = prior[h]

        @pl.when(pair > 0)
        def _():
            z_copy(i).wait_recv()

        s_copy(i).wait_recv()
        came = enter[i]
        a, b = own[h], cross[i]
        da, db = dec[pl.ds(h, 1), :], dec_x[pl.ds(h, 1), :]
        mid = jnp.where(first, da, db) * came + jnp.where(first, a, b)
        pass_z[i] = jnp.where(first, db, da) * mid + jnp.where(first, b, a)

        @pl.when(pair < last)
        def _():
            z_copy(i).start()

        pass_x[i] = jnp.where(first, mid, came)
        x_copy(i).start()
        state = jnp.where(first, came, mid)
        used[h] = state
        finish(h, state)

    @pl.loop(0, half)
    def _(i):
        x_copy(i).wait_recv()
        state = part[i]
        used[theirs + i] = state
        finish(theirs + i, state)

    sums[...] = jnp.zeros_like(sums)
    sums[0:1, :] = jnp.sum(sq_acc[...].T, axis=0, keepdims=True)
    sums[1:2, :] = jnp.sum(rd_acc[...].T, axis=0, keepdims=True)
    for copy in sum_copies:
        copy.start()
    total = sums[...]
    for d, copy in enumerate(sum_copies):
        copy.wait_recv()
        total = total + sums_in[d]
    inv_row = lax.rsqrt(total[0:1, :] / D + epsilon)
    coef_row = inv_row * inv_row * inv_row * total[1:2, :] / D
    sq_acc[...] = jnp.broadcast_to(inv_row, (HD, BLK)).T
    rd_acc[...] = jnp.broadcast_to(coef_row, (HD, BLK)).T

    def gradient(h):
        g = (sq_acc[...] * gnorm[h] - ctx[h] * rd_acc[...]).astype(BF16)
        grad[h] = g
        scaled = (q[:, cols(h)].astype(F32) * jnp.exp(run_col[h])).astype(BF16)
        own_b[h] = dot(scaled, g, 0, 0)

    @pl.loop(0, half)
    def _(i):
        gradient(theirs + i)
        bs_copy(i).start()

    def local_back(h):
        g, w = grad[h], wts[h]
        gm = (dot(g, v[:, cols(h)], 1, 1) * w).astype(BF16)
        gq[:, cols(h)] = (
            dot(gm, k[:, cols(h)], 1, 0) + jnp.exp(run_col[h]) * dot(g, used[h].astype(BF16), 1, 1)
        ).astype(BF16)
        gk_acc[h] = dot(gm, q[:, cols(h)], 0, 0)
        gv_acc[h] = dot(mix[h], g, 0, 0)
        normed = ctx[h] * sq_acc[...]
        opened = jax.nn.sigmoid(gate[:, cols(h)].astype(F32))
        att[:, cols(h)] = (normed * gain_ref[:, cols(h)] * opened).astype(BF16)
        gg[:, cols(h)] = (gnorm[h] * normed * (1.0 - opened)).astype(BF16)

    def finish_back(h, state):
        remain = remain_of(h)
        s = state.astype(BF16)
        gk[:, cols(h)] = (gk_acc[h] + remain * dot(v[:, cols(h)], s, 1, 1)).astype(BF16)
        gv[:, cols(h)] = (gv_acc[h] + remain * dot(k[:, cols(h)], s, 1, 0)).astype(BF16)

    @pl.loop(0, half)
    def _(i):
        h = mine + i
        gradient(h)
        local_back(h)
        local_back(theirs + i)

        @pl.when(pair == last)
        def _():
            enter_b[i] = jnp.zeros((HD, HD), F32)

        @pl.when(pair < last)
        def _():
            bz_copy(i).wait_recv()

        bs_copy(i).wait_recv()
        came = enter_b[i]
        a, b = own_b[h], cross_b[i]
        da, db = dec[pl.ds(h, 1), :], dec_x[pl.ds(h, 1), :]
        mid = jnp.where(first, db, da) * came + jnp.where(first, b, a)
        pass_z_b[i] = jnp.where(first, da, db) * mid + jnp.where(first, a, b)

        @pl.when(pair > 0)
        def _():
            bz_copy(i).start()

        pass_x_b[i] = jnp.where(first, came, mid)
        bx_copy(i).start()
        finish_back(h, jnp.where(first, mid, came))

    stores = [
        pltpu.make_async_copy(src, dst, out_sem.at[j])
        for j, (src, dst) in enumerate(
            [(att, att_hbm), (gq, gq_hbm), (gg, gg_hbm), (gk, gk_hbm), (gv, gv_hbm)]
        )
    ]
    for store in stores[:3]:
        store.start()

    @pl.loop(0, half)
    def _(i):
        bx_copy(i).wait_recv()
        finish_back(theirs + i, part_b[i])

    for store in stores[3:]:
        store.start()

    dec_copy.wait_send()
    for copy in sum_copies:
        copy.wait_send()

    @pl.loop(0, half)
    def _(i):
        s_copy(i).wait_send()
        x_copy(i).wait_send()
        bs_copy(i).wait_send()
        bx_copy(i).wait_send()

        @pl.when(pair < last)
        def _():
            z_copy(i).wait_send()

        @pl.when(pair > 0)
        def _():
            bz_copy(i).wait_send()

    for store in stores:
        store.wait()


def solution(mesh):
    n_seq, n_head = mesh.shape["seq"], mesh.shape["head"]

    def shards(queries, key_rows, value_rows, log_decay, gate_input, out_gain, prior_state, out_grad):
        length, features = queries.shape
        heads = log_decay.shape[1]
        half = heads // 2
        wide = (length, features)
        anywhere = pl.BlockSpec(memory_space=pl.ANY)
        vmem = pl.BlockSpec(memory_space=pltpu.VMEM)

        def states(count):
            return pltpu.VMEM((count, HD, HD), F32)

        dma = pltpu.SemaphoreType.DMA
        return pl.pallas_call(
            functools.partial(kernel, n_seq, n_head, heads),
            out_shape=[jax.ShapeDtypeStruct(wide, BF16)] * 5,
            in_specs=[anywhere, anywhere, anywhere, vmem, anywhere, vmem, anywhere, anywhere],
            out_specs=[anywhere] * 5,
            scratch_shapes=[pltpu.VMEM(wide, BF16)] * 5
            + [states(heads)]
            + [pltpu.VMEM(wide, BF16)] * 5
            + [
                pltpu.VMEM((heads, BLK, HD), F32),
                pltpu.VMEM((heads, BLK), F32),
                pltpu.VMEM((heads, HD), F32),
                pltpu.VMEM((heads, HD), F32),
            ]
            + [states(heads)] + [states(half)] * 5 + [states(heads)]
            + [states(heads)] + [states(half)] * 5
            + [
                pltpu.VMEM((heads, BLK, BLK), F32),
                pltpu.VMEM((heads, BLK, BLK), BF16),
                pltpu.VMEM((heads, BLK, HD), F32),
                pltpu.VMEM((heads, BLK, HD), F32),
                pltpu.VMEM((heads, BLK, HD), BF16),
                pltpu.VMEM((heads, BLK, HD), F32),
                pltpu.VMEM((heads, BLK, HD), F32),
                pltpu.VMEM((BLK, HD), F32),
                pltpu.VMEM((BLK, HD), F32),
                pltpu.VMEM((8, BLK), F32),
                pltpu.VMEM((n_head - 1, 8, BLK), F32),
                dma((6,)),
                dma((5,)),
                dma,
                dma,
                dma((n_head - 1,)),
                dma((n_head - 1,)),
            ]
            + [dma((half,))] * 12,
            compiler_params=pltpu.CompilerParams(
                collective_id=0, has_side_effects=True, vmem_limit_bytes=56 * 1024 * 1024
            ),
            cost_estimate=pl.CostEstimate(
                flops=4_000_000_000, bytes_accessed=12_000_000, transcendentals=2_000_000
            ),
        )(
            queries, key_rows, value_rows, log_decay, gate_input,
            out_gain.reshape(1, features), prior_state, out_grad,
        )

    cut = P("seq", "head")
    return jax.shard_map(
        shards,
        mesh=mesh,
        in_specs=(cut, cut, cut, cut, cut, P("head"), P("head", None, None), cut),
        out_specs=(cut,) * 5,
        check_vma=False,
    )
```

```python
import functools

import jax
import jax.numpy as jnp
from jax import lax
from jax.experimental import pallas as pl
from jax.experimental.pallas import tpu as pltpu
from jax.sharding import PartitionSpec as P

BLK = 256
D = 8192
HD = 128
PARTS = 2
LAG = 2
ROWS = HD // PARTS
epsilon = 1e-06
MESH = pl.DeviceIdType.MESH
F32 = jnp.float32
BF16 = jnp.bfloat16


def dot(a, b, ca, cb):
    return lax.dot_general(a, b, (((ca,), (cb,)), ((), ())), preferred_element_type=F32)


def kernel(
    n_seq, n_head, heads,
    q_hbm, k_hbm, v_hbm, ld_ref, gate_hbm, gain_ref, prior_hbm, og_hbm,
    att_hbm, gq_hbm, gk_hbm, gv_hbm, gg_hbm,
    q, k, v, gate, og, prior,
    att, gq, gk, gv, gg,
    run_col, run_row, dec, dec_x,
    own, cross, enter, part, pass_z, pass_x, used,
    own_b, cross_b, enter_b, part_b, pass_z_b, pass_x_b, used_b,
    wts, mix, ctx, gnorm, grad, gk_acc, gv_acc,
    sq_acc, rd_acc, sums, sums_in,
    in_sem, out_sem, dec_send, dec_recv, sum_send, sum_recv,
    s_send, s_recv, z_send, z_recv, x_send, x_recv,
    bs_send, bs_recv, bz_send, bz_recv, bx_send, bx_recv,
):
    half = heads // 2
    me = lax.axis_index("seq")
    row = lax.axis_index("head")
    pair, side = me // 2, me % 2
    last = n_seq // 2 - 1
    partner = me + 1 - 2 * side
    mine, theirs = side * half, (1 - side) * half

    barrier = pltpu.get_barrier_semaphore()

    def greet(**target):
        pl.semaphore_signal(barrier, inc=1, device_id=target, device_id_type=MESH)

    greet(seq=partner)
    for d in range(1, n_head):
        greet(head=lax.rem(row + d, n_head))

    @pl.when(pair > 0)
    def _():
        greet(seq=me - 2)

    @pl.when(pair < last)
    def _():
        greet(seq=me + 2)

    loads = [
        pltpu.make_async_copy(src, dst, in_sem.at[j])
        for j, (src, dst) in enumerate(
            [(k_hbm, k), (v_hbm, v), (q_hbm, q), (gate_hbm, gate), (og_hbm, og), (prior_hbm, prior)]
        )
    ]
    for load in loads:
        load.start()

    ti = lax.broadcasted_iota(jnp.int32, (BLK, BLK), 0)
    si = lax.broadcasted_iota(jnp.int32, (BLK, BLK), 1)
    causal = ti >= si
    low = jnp.where(causal, 1.0, 0.0).astype(F32)
    ld = ld_ref[...]
    col = lax.dot_general(
        low, ld, (((1,), (1,)), ((), ())), precision=lax.Precision.HIGHEST, preferred_element_type=F32
    )
    run_row[...] = lax.dot_general(
        ld, low, (((1,), (1,)), ((), ())), precision=lax.Precision.HIGHEST, preferred_element_type=F32
    )
    for h in range(heads):
        wide = jnp.broadcast_to(col[:, h : h + 1], (BLK, HD))
        run_col[h] = wide
        dec[h : h + 1, :] = jnp.exp(wide[BLK - 1 : BLK, :])

    def cols(h):
        return pl.ds(pl.multiple_of(h * HD, HD), HD)

    def send(src, dst, s, r, **target):
        return pltpu.make_async_remote_copy(
            src_ref=src, dst_ref=dst, send_sem=s, recv_sem=r, device_id=target, device_id_type=MESH
        )

    sum_copies = [
        send(sums, sums_in.at[d - 1], sum_send.at[d - 1], sum_recv.at[d - 1], head=lax.rem(row + d, n_head))
        for d in range(1, n_head)
    ]
    dec_copy = send(dec, dec_x, dec_send, dec_recv, seq=partner)

    def piece(ref, i, j):
        return ref.at[i, pl.ds(j * ROWS, ROWS)]

    def s_copy(i, j):
        n = i * PARTS + j
        return send(piece(own, theirs + i, j), piece(cross, i, j), s_send.at[n], s_recv.at[n], seq=partner)

    def z_copy(i, j):
        n = i * PARTS + j
        return send(piece(pass_z, i, j), piece(enter, i, j), z_send.at[n], z_recv.at[n], seq=me + 2)

    def x_copy(i, j):
        n = i * PARTS + j
        return send(piece(pass_x, i, j), piece(part, i, j), x_send.at[n], x_recv.at[n], seq=partner)

    def bs_copy(i, j):
        n = i * PARTS + j
        return send(piece(own_b, theirs + i, j), piece(cross_b, i, j), bs_send.at[n], bs_recv.at[n], seq=partner)

    def bz_copy(i, j):
        n = i * PARTS + j
        return send(piece(pass_z_b, i, j), piece(enter_b, i, j), bz_send.at[n], bz_recv.at[n], seq=me - 2)

    def bx_copy(i, j):
        n = i * PARTS + j
        return send(piece(pass_x_b, i, j), piece(part_b, i, j), bx_send.at[n], bx_recv.at[n], seq=partner)

    def remain_of(h):
        wide = run_col[h]
        return jnp.exp(wide[BLK - 1 : BLK, :] - wide)

    def summary(h):
        scaled = (k[:, cols(h)].astype(F32) * remain_of(h)).astype(BF16)
        own[h] = dot(scaled, v[:, cols(h)], 0, 0)

    loads[0].wait()
    loads[1].wait()
    pl.semaphore_wait(
        barrier, n_head + jnp.where(pair > 0, 1, 0) + jnp.where(pair < last, 1, 0)
    )
    dec_copy.start()

    @pl.loop(0, half)
    def _(i):
        summary(theirs + i)
        for j in range(PARTS):
            s_copy(i, j).start()

    for load in loads[2:]:
        load.wait()
    dec_copy.wait_recv()
    sq_acc[...] = jnp.zeros_like(sq_acc)
    rd_acc[...] = jnp.zeros_like(rd_acc)

    def within(h):
        spread = jnp.broadcast_to(run_col[h][:, :1], (BLK, BLK)) - run_row[pl.ds(h, 1), :]
        w = jnp.where(causal, jnp.exp(jnp.minimum(spread, 0.0)), 0.0)
        wts[h] = w
        m = (dot(q[:, cols(h)], k[:, cols(h)], 1, 1) * w).astype(BF16)
        mix[h] = m
        ctx[h] = dot(m, v[:, cols(h)], 1, 0)
        opened = jax.nn.sigmoid(gate[:, cols(h)].astype(F32))
        gnorm[h] = og[:, cols(h)].astype(F32) * gain_ref[:, cols(h)] * opened

    def finish(h, state):
        c = ctx[h] + jnp.exp(run_col[h]) * dot(q[:, cols(h)], state.astype(BF16), 1, 0)
        ctx[h] = c
        sq_acc[...] += c * c
        rd_acc[...] += c * gnorm[h]

    first = side == 0

    def chain(i):
        h = mine + i
        da, db = dec[pl.ds(h, 1), :], dec_x[pl.ds(h, 1), :]
        d0, d1 = jnp.where(first, da, db), jnp.where(first, db, da)
        for j in range(PARTS):
            rows = pl.ds(j * ROWS, ROWS)
            s_copy(i, j).wait_recv()

            @pl.when(pair == 0)
            def _():
                enter[i, rows] = prior[h, rows]

            @pl.when(pair > 0)
            def _():
                z_copy(i, j).wait_recv()

            came = enter[i, rows]
            a, b = own[h, rows], cross[i, rows]
            mid = d0 * came + jnp.where(first, a, b)
            pass_z[i, rows] = d1 * mid + jnp.where(first, b, a)

            @pl.when(pair < last)
            def _():
                z_copy(i, j).start()

            pass_x[i, rows] = jnp.where(first, mid, came)
            x_copy(i, j).start()
            used[h, rows] = jnp.where(first, came, mid)

    def receive(i):
        for j in range(PARTS):
            x_copy(i, j).wait_recv()
        used[theirs + i] = part[i]
        finish(theirs + i, part[i])

    @pl.loop(0, half + last + LAG)
    def _(t):
        step = t - pair
        active = jnp.logical_and(step >= 0, step < half)

        @pl.when(t < half)
        def _():
            summary(mine + t)

        @pl.when(active)
        def _():
            chain(step)

        @pl.when(t < half)
        def _():
            within(mine + t)
            within(theirs + t)

        @pl.when(active)
        def _():
            finish(mine + step, used[mine + step])

        late = step - LAG

        @pl.when(jnp.logical_and(late >= 0, late < half))
        def _():
            receive(late)

    sums[...] = jnp.zeros_like(sums)
    sums[0:1, :] = jnp.sum(sq_acc[...].T, axis=0, keepdims=True)
    sums[1:2, :] = jnp.sum(rd_acc[...].T, axis=0, keepdims=True)
    for copy in sum_copies:
        copy.start()
    total = sums[...]
    for d, copy in enumerate(sum_copies):
        copy.wait_recv()
        total = total + sums_in[d]
    inv_row = lax.rsqrt(total[0:1, :] / D + epsilon)
    coef_row = inv_row * inv_row * inv_row * total[1:2, :] / D
    sq_acc[...] = jnp.broadcast_to(inv_row, (HD, BLK)).T
    rd_acc[...] = jnp.broadcast_to(coef_row, (HD, BLK)).T

    def gradient(h):
        g = (sq_acc[...] * gnorm[h] - ctx[h] * rd_acc[...]).astype(BF16)
        grad[h] = g
        scaled = (q[:, cols(h)].astype(F32) * jnp.exp(run_col[h])).astype(BF16)
        own_b[h] = dot(scaled, g, 0, 0)

    @pl.loop(0, half)
    def _(i):
        gradient(theirs + i)
        for j in range(PARTS):
            bs_copy(i, j).start()

    def local_back(h):
        g, w = grad[h], wts[h]
        gm = (dot(g, v[:, cols(h)], 1, 1) * w).astype(BF16)
        gq[:, cols(h)] = (
            dot(gm, k[:, cols(h)], 1, 0) + jnp.exp(run_col[h]) * dot(g, used[h].astype(BF16), 1, 1)
        ).astype(BF16)
        gk_acc[h] = dot(gm, q[:, cols(h)], 0, 0)
        gv_acc[h] = dot(mix[h], g, 0, 0)
        normed = ctx[h] * sq_acc[...]
        opened = jax.nn.sigmoid(gate[:, cols(h)].astype(F32))
        att[:, cols(h)] = (normed * gain_ref[:, cols(h)] * opened).astype(BF16)
        gg[:, cols(h)] = (gnorm[h] * normed * (1.0 - opened)).astype(BF16)

    def finish_back(h, state):
        remain = remain_of(h)
        s = state.astype(BF16)
        gk[:, cols(h)] = (gk_acc[h] + remain * dot(v[:, cols(h)], s, 1, 1)).astype(BF16)
        gv[:, cols(h)] = (gv_acc[h] + remain * dot(k[:, cols(h)], s, 1, 0)).astype(BF16)

    def chain_back(i):
        h = mine + i
        da, db = dec[pl.ds(h, 1), :], dec_x[pl.ds(h, 1), :]
        d0, d1 = jnp.where(first, da, db), jnp.where(first, db, da)
        for j in range(PARTS):
            rows = pl.ds(j * ROWS, ROWS)
            bs_copy(i, j).wait_recv()

            @pl.when(pair == last)
            def _():
                enter_b[i, rows] = jnp.zeros((ROWS, HD), F32)

            @pl.when(pair < last)
            def _():
                bz_copy(i, j).wait_recv()

            came = enter_b[i, rows]
            a, b = own_b[h, rows], cross_b[i, rows]
            mid = d1 * came + jnp.where(first, b, a)
            pass_z_b[i, rows] = d0 * mid + jnp.where(first, a, b)

            @pl.when(pair > 0)
            def _():
                bz_copy(i, j).start()

            pass_x_b[i, rows] = jnp.where(first, came, mid)
            bx_copy(i, j).start()
            used_b[i, rows] = jnp.where(first, mid, came)

    @pl.loop(0, half + last + LAG)
    def _(t):
        step = t - (last - pair)
        active = jnp.logical_and(step >= 0, step < half)

        @pl.when(t < half)
        def _():
            gradient(mine + t)

        @pl.when(active)
        def _():
            chain_back(step)

        @pl.when(t < half)
        def _():
            local_back(mine + t)
            local_back(theirs + t)

        @pl.when(active)
        def _():
            finish_back(mine + step, used_b[step])

        late = step - LAG

        @pl.when(jnp.logical_and(late >= 0, late < half))
        def _():
            for j in range(PARTS):
                bx_copy(late, j).wait_recv()
            finish_back(theirs + late, part_b[late])

    stores = [
        pltpu.make_async_copy(src, dst, out_sem.at[j])
        for j, (src, dst) in enumerate(
            [(att, att_hbm), (gq, gq_hbm), (gg, gg_hbm), (gk, gk_hbm), (gv, gv_hbm)]
        )
    ]
    for store in stores:
        store.start()

    dec_copy.wait_send()
    for copy in sum_copies:
        copy.wait_send()

    @pl.loop(0, half)
    def _(i):
        for j in range(PARTS):
            s_copy(i, j).wait_send()
            x_copy(i, j).wait_send()
            bs_copy(i, j).wait_send()
            bx_copy(i, j).wait_send()

            @pl.when(pair < last)
            def _():
                z_copy(i, j).wait_send()

            @pl.when(pair > 0)
            def _():
                bz_copy(i, j).wait_send()

    for store in stores:
        store.wait()


def deliver(rows, *refs):
    sources, targets, staged, (in_sem, out_sem) = refs[:5], refs[5:10], refs[10:15], refs[15:]
    loads, stores = [], []
    for j in range(10):
        part = pl.ds(j // 5 * rows, rows)
        a, b, c = sources[j % 5].at[part], staged[j % 5].at[part], targets[j % 5].at[part]
        loads.append(pltpu.make_async_copy(a, b, in_sem.at[j]))
        stores.append(pltpu.make_async_copy(b, c, out_sem.at[j]))
    for load in loads:
        load.start()
    for load, store in zip(loads, stores):
        load.wait()
        store.start()
    for store in stores:
        store.wait()


def solution(mesh):
    n_seq, n_head = mesh.shape["seq"], mesh.shape["head"]

    def shards(queries, key_rows, value_rows, log_decay, gate_input, out_gain, prior_state, out_grad):
        length, features = queries.shape
        heads = log_decay.shape[1]
        half = heads // 2
        wide = (length, features)
        anywhere = pl.BlockSpec(memory_space=pl.ANY)
        vmem = pl.BlockSpec(memory_space=pltpu.VMEM)

        def states(count):
            return pltpu.VMEM((count, HD, HD), F32)

        dma = pltpu.SemaphoreType.DMA
        results = pl.pallas_call(
            functools.partial(kernel, n_seq, n_head, heads),
            out_shape=[jax.ShapeDtypeStruct(wide, BF16)] * 5,
            in_specs=[anywhere, anywhere, anywhere, vmem, anywhere, vmem, anywhere, anywhere],
            out_specs=[anywhere] * 5,
            scratch_shapes=[pltpu.VMEM(wide, BF16)] * 5
            + [states(heads)]
            + [pltpu.VMEM(wide, BF16)] * 5
            + [
                pltpu.VMEM((heads, BLK, HD), F32),
                pltpu.VMEM((heads, BLK), F32),
                pltpu.VMEM((heads, HD), F32),
                pltpu.VMEM((heads, HD), F32),
            ]
            + [states(heads)] + [states(half)] * 5 + [states(heads)]
            + [states(heads)] + [states(half)] * 6
            + [
                pltpu.VMEM((heads, BLK, BLK), F32),
                pltpu.VMEM((heads, BLK, BLK), BF16),
                pltpu.VMEM((heads, BLK, HD), F32),
                pltpu.VMEM((heads, BLK, HD), F32),
                pltpu.VMEM((heads, BLK, HD), BF16),
                pltpu.VMEM((heads, BLK, HD), F32),
                pltpu.VMEM((heads, BLK, HD), F32),
                pltpu.VMEM((BLK, HD), F32),
                pltpu.VMEM((BLK, HD), F32),
                pltpu.VMEM((8, BLK), F32),
                pltpu.VMEM((n_head - 1, 8, BLK), F32),
                dma((6,)),
                dma((5,)),
                dma,
                dma,
                dma((n_head - 1,)),
                dma((n_head - 1,)),
            ]
            + [dma((half * PARTS,))] * 12,
            compiler_params=pltpu.CompilerParams(
                collective_id=0, has_side_effects=True, vmem_limit_bytes=56 * 1024 * 1024
            ),
            cost_estimate=pl.CostEstimate(
                flops=4_000_000_000, bytes_accessed=12_000_000, transcendentals=2_000_000
            ),
        )(
            queries, key_rows, value_rows, log_decay.T, gate_input,
            out_gain.reshape(1, features), prior_state, out_grad,
        )
        return pl.pallas_call(
            functools.partial(deliver, length // 2),
            out_shape=[jax.ShapeDtypeStruct(wide, BF16)] * 5,
            in_specs=[anywhere] * 5,
            out_specs=[anywhere] * 5,
            scratch_shapes=[pltpu.VMEM(wide, BF16)] * 5 + [dma((10,)), dma((10,))],
            compiler_params=pltpu.CompilerParams(vmem_limit_bytes=60 * 1024 * 1024),
            cost_estimate=pl.CostEstimate(flops=0, bytes_accessed=10_000_000, transcendentals=0),
        )(*results)

    cut = P("seq", "head")
    return jax.shard_map(
        shards,
        mesh=mesh,
        in_specs=(cut, cut, cut, cut, cut, P("head"), P("head", None, None), cut),
        out_specs=(cut,) * 5,
        check_vma=False,
    )
```

```python
import functools

import jax
import jax.numpy as jnp
from jax import lax
from jax.experimental import pallas as pl
from jax.experimental.pallas import tpu as pltpu
from jax.sharding import PartitionSpec as P

BLK = 256
D = 8192
HD = 128
PARTS = 1
LAG = 1
GROUP = 2
ROWS = HD // PARTS
epsilon = 1e-06
MESH = pl.DeviceIdType.MESH
F32 = jnp.float32
BF16 = jnp.bfloat16


def dot(a, b, ca, cb):
    return lax.dot_general(a, b, (((ca,), (cb,)), ((), ())), preferred_element_type=F32)


def kernel(
    n_seq, n_head, heads,
    q_hbm, k_hbm, v_hbm, ld_ref, gate_hbm, gain_ref, prior_hbm, og_hbm,
    att, gq, gk, gv, gg,
    q, k, v, gate, og, prior,
    run_col, run_row, dec, dec_x,
    own, cross, enter, part, pass_z, pass_x, used,
    own_b, cross_b, enter_b, part_b, pass_z_b, pass_x_b, used_b,
    wts, mix, ctx, gnorm, grad, gk_acc, gv_acc,
    sq_acc, rd_acc, sums, sums_in,
    in_sem, dec_send, dec_recv, sum_send, sum_recv,
    s_send, s_recv, z_send, z_recv, x_send, x_recv,
    bs_send, bs_recv, bz_send, bz_recv, bx_send, bx_recv,
):
    half = heads // 2
    me = lax.axis_index("seq")
    row = lax.axis_index("head")
    pair, side = me // 2, me % 2
    last = n_seq // 2 - 1
    partner = me + 1 - 2 * side
    mine, theirs = side * half, (1 - side) * half

    barrier = pltpu.get_barrier_semaphore()

    def greet(**target):
        pl.semaphore_signal(barrier, inc=1, device_id=target, device_id_type=MESH)

    greet(seq=partner)
    for d in range(1, n_head):
        greet(head=lax.rem(row + d, n_head))

    @pl.when(pair > 0)
    def _():
        greet(seq=me - 2)

    @pl.when(pair < last)
    def _():
        greet(seq=me + 2)

    loads = [
        pltpu.make_async_copy(src, dst, in_sem.at[j])
        for j, (src, dst) in enumerate(
            [(k_hbm, k), (v_hbm, v), (q_hbm, q), (gate_hbm, gate), (og_hbm, og), (prior_hbm, prior)]
        )
    ]
    for load in loads:
        load.start()

    ti = lax.broadcasted_iota(jnp.int32, (BLK, BLK), 0)
    si = lax.broadcasted_iota(jnp.int32, (BLK, BLK), 1)
    causal = ti >= si
    low = jnp.where(causal, 1.0, 0.0).astype(F32)
    ld = ld_ref[...]
    col = lax.dot_general(
        low, ld, (((1,), (1,)), ((), ())), precision=lax.Precision.HIGHEST, preferred_element_type=F32
    )
    run_row[...] = lax.dot_general(
        ld, low, (((1,), (1,)), ((), ())), precision=lax.Precision.HIGHEST, preferred_element_type=F32
    )
    for h in range(heads):
        wide = jnp.broadcast_to(col[:, h : h + 1], (BLK, HD))
        run_col[h] = wide
        dec[h : h + 1, :] = jnp.exp(wide[BLK - 1 : BLK, :])

    def cols(h):
        return pl.ds(pl.multiple_of(h * HD, HD), HD)

    def send(src, dst, s, r, **target):
        return pltpu.make_async_remote_copy(
            src_ref=src, dst_ref=dst, send_sem=s, recv_sem=r, device_id=target, device_id_type=MESH
        )

    sum_copies = [
        send(sums, sums_in.at[d - 1], sum_send.at[d - 1], sum_recv.at[d - 1], head=lax.rem(row + d, n_head))
        for d in range(1, n_head)
    ]
    dec_copy = send(dec, dec_x, dec_send, dec_recv, seq=partner)

    def piece(ref, i, j):
        return ref.at[i, pl.ds(j * ROWS, ROWS)]

    def s_copy(i, j):
        n = i * PARTS + j
        return send(piece(own, theirs + i, j), piece(cross, i, j), s_send.at[n], s_recv.at[n], seq=partner)

    def z_copy(i, j):
        n = i * PARTS + j
        return send(piece(pass_z, i, j), piece(enter, i, j), z_send.at[n], z_recv.at[n], seq=me + 2)

    def x_copy(i, j):
        n = i * PARTS + j
        return send(piece(pass_x, i, j), piece(part, i, j), x_send.at[n], x_recv.at[n], seq=partner)

    def bs_copy(i, j):
        n = i * PARTS + j
        return send(piece(own_b, theirs + i, j), piece(cross_b, i, j), bs_send.at[n], bs_recv.at[n], seq=partner)

    def bz_copy(i, j):
        n = i * PARTS + j
        return send(piece(pass_z_b, i, j), piece(enter_b, i, j), bz_send.at[n], bz_recv.at[n], seq=me - 2)

    def bx_copy(i, j):
        n = i * PARTS + j
        return send(piece(pass_x_b, i, j), piece(part_b, i, j), bx_send.at[n], bx_recv.at[n], seq=partner)

    def remain_of(h):
        wide = run_col[h]
        return jnp.exp(wide[BLK - 1 : BLK, :] - wide)

    def summaries(hs):
        scaled = [(k[:, cols(h)].astype(F32) * remain_of(h)).astype(BF16) for h in hs]
        made = [dot(a, v[:, cols(h)], 0, 0) for a, h in zip(scaled, hs)]
        for h, state in zip(hs, made):
            own[h] = state

    loads[0].wait()
    loads[1].wait()
    pl.semaphore_wait(
        barrier, n_head + jnp.where(pair > 0, 1, 0) + jnp.where(pair < last, 1, 0)
    )
    dec_copy.start()

    def spread_of(start, g):
        return [start + g * GROUP + i for i in range(GROUP)]

    groups = half // GROUP

    @pl.loop(0, groups)
    def _(g):
        summaries(spread_of(theirs, g))
        for i in spread_of(0, g):
            for j in range(PARTS):
                s_copy(i, j).start()

    @pl.loop(0, groups)
    def _(g):
        summaries(spread_of(mine, g))

    for load in loads[2:]:
        load.wait()
    dec_copy.wait_recv()
    sq_acc[...] = jnp.zeros_like(sq_acc)
    rd_acc[...] = jnp.zeros_like(rd_acc)

    def within(hs):
        scores = [dot(q[:, cols(h)], k[:, cols(h)], 1, 1) for h in hs]
        ws = []
        for h in hs:
            wide = run_col[h]
            spread = jnp.concatenate([wide, wide], axis=1) - run_row[pl.ds(h, 1), :]
            ws.append(jnp.where(causal, jnp.exp(jnp.minimum(spread, 0.0)), 0.0))
        ms = [(a * w).astype(BF16) for a, w in zip(scores, ws)]
        rows = [dot(m, v[:, cols(h)], 1, 0) for m, h in zip(ms, hs)]
        opens = [jax.nn.sigmoid(gate[:, cols(h)].astype(F32)) for h in hs]
        norms = [og[:, cols(h)].astype(F32) * gain_ref[:, cols(h)] * o for h, o in zip(hs, opens)]
        for h, w, m, c, o in zip(hs, ws, ms, rows, norms):
            wts[h] = w
            mix[h] = m
            ctx[h] = c
            gnorm[h] = o

    def finish(hs):
        across = [dot(q[:, cols(h)], used[h].astype(BF16), 1, 0) for h in hs]
        cs = [ctx[h] + jnp.exp(run_col[h]) * a for h, a in zip(hs, across)]
        squares, dots = sq_acc[...], rd_acc[...]
        for h, c in zip(hs, cs):
            squares = squares + c * c
            dots = dots + c * gnorm[h]
        for h, c in zip(hs, cs):
            ctx[h] = c
        sq_acc[...] = squares
        rd_acc[...] = dots

    first = side == 0

    def chain(i):
        h = mine + i
        da, db = dec[pl.ds(h, 1), :], dec_x[pl.ds(h, 1), :]
        d0, d1 = jnp.where(first, da, db), jnp.where(first, db, da)
        for j in range(PARTS):
            rows = pl.ds(j * ROWS, ROWS)
            s_copy(i, j).wait_recv()

            @pl.when(pair == 0)
            def _():
                enter[i, rows] = prior[h, rows]

            @pl.when(pair > 0)
            def _():
                z_copy(i, j).wait_recv()

            came = enter[i, rows]
            a, b = own[h, rows], cross[i, rows]
            mid = d0 * came + jnp.where(first, a, b)
            pass_z[i, rows] = d1 * mid + jnp.where(first, b, a)

            @pl.when(pair < last)
            def _():
                z_copy(i, j).start()

            pass_x[i, rows] = jnp.where(first, mid, came)
            x_copy(i, j).start()
            used[h, rows] = jnp.where(first, came, mid)

    @pl.loop(0, groups + last + LAG)
    def _(t):
        step = t - pair
        active = jnp.logical_and(step >= 0, step < groups)
        late = step - LAG

        @pl.when(active)
        def _():
            for i in spread_of(0, step):
                chain(i)

        @pl.when(t < groups)
        def _():
            within(spread_of(mine, t) + spread_of(theirs, t))

        @pl.when(active)
        def _():
            finish(spread_of(mine, step))

        @pl.when(jnp.logical_and(late >= 0, late < groups))
        def _():
            for i in spread_of(0, late):
                for j in range(PARTS):
                    x_copy(i, j).wait_recv()
                used[theirs + i] = part[i]
            finish(spread_of(theirs, late))

    sums[...] = jnp.zeros_like(sums)
    sums[0:1, :] = jnp.sum(sq_acc[...].T, axis=0, keepdims=True)
    sums[1:2, :] = jnp.sum(rd_acc[...].T, axis=0, keepdims=True)
    for copy in sum_copies:
        copy.start()
    total = sums[...]
    for d, copy in enumerate(sum_copies):
        copy.wait_recv()
        total = total + sums_in[d]
    inv_row = lax.rsqrt(total[0:1, :] / D + epsilon)
    coef_row = inv_row * inv_row * inv_row * total[1:2, :] / D
    sq_acc[...] = jnp.broadcast_to(inv_row, (HD, BLK)).T
    rd_acc[...] = jnp.broadcast_to(coef_row, (HD, BLK)).T

    def gradients(hs):
        inv, coef = sq_acc[...], rd_acc[...]
        gs = [(inv * gnorm[h] - ctx[h] * coef).astype(BF16) for h in hs]
        scaled = [(q[:, cols(h)].astype(F32) * jnp.exp(run_col[h])).astype(BF16) for h in hs]
        made = [dot(a, g, 0, 0) for a, g in zip(scaled, gs)]
        for h, g, state in zip(hs, gs, made):
            grad[h] = g
            own_b[h] = state

    @pl.loop(0, groups)
    def _(g):
        gradients(spread_of(theirs, g))
        for i in spread_of(0, g):
            for j in range(PARTS):
                bs_copy(i, j).start()

    @pl.loop(0, groups)
    def _(g):
        gradients(spread_of(mine, g))

    def local_back(hs):
        gs = [grad[h] for h in hs]
        scores = [dot(g, v[:, cols(h)], 1, 1) for g, h in zip(gs, hs)]
        across = [dot(g, used[h].astype(BF16), 1, 1) for g, h in zip(gs, hs)]
        values = [dot(mix[h], g, 0, 0) for g, h in zip(gs, hs)]
        gms = [(a * wts[h]).astype(BF16) for a, h in zip(scores, hs)]
        queries = [dot(m, k[:, cols(h)], 1, 0) for m, h in zip(gms, hs)]
        keys = [dot(m, q[:, cols(h)], 0, 0) for m, h in zip(gms, hs)]
        queries = [
            (a + jnp.exp(run_col[h]) * b).astype(BF16) for a, b, h in zip(queries, across, hs)
        ]
        outs = []
        for h in hs:
            normed = ctx[h] * sq_acc[...]
            opened = jax.nn.sigmoid(gate[:, cols(h)].astype(F32))
            outs.append(
                (
                    (normed * gain_ref[:, cols(h)] * opened).astype(BF16),
                    (gnorm[h] * normed * (1.0 - opened)).astype(BF16),
                )
            )
        for h, a, b, c, (d, e) in zip(hs, queries, keys, values, outs):
            gq[:, cols(h)] = a
            gk_acc[h] = b
            gv_acc[h] = c
            att[:, cols(h)] = d
            gg[:, cols(h)] = e

    def finish_back(hs, states):
        states = [state.astype(BF16) for state in states]
        keys = [dot(v[:, cols(h)], a, 1, 1) for h, a in zip(hs, states)]
        values = [dot(k[:, cols(h)], a, 1, 0) for h, a in zip(hs, states)]
        done = []
        for h, a, b in zip(hs, keys, values):
            remain = remain_of(h)
            done.append(((gk_acc[h] + remain * a).astype(BF16), (gv_acc[h] + remain * b).astype(BF16)))
        for h, (a, b) in zip(hs, done):
            gk[:, cols(h)] = a
            gv[:, cols(h)] = b

    def chain_back(i):
        h = mine + i
        da, db = dec[pl.ds(h, 1), :], dec_x[pl.ds(h, 1), :]
        d0, d1 = jnp.where(first, da, db), jnp.where(first, db, da)
        for j in range(PARTS):
            rows = pl.ds(j * ROWS, ROWS)
            bs_copy(i, j).wait_recv()

            @pl.when(pair == last)
            def _():
                enter_b[i, rows] = jnp.zeros((ROWS, HD), F32)

            @pl.when(pair < last)
            def _():
                bz_copy(i, j).wait_recv()

            came = enter_b[i, rows]
            a, b = own_b[h, rows], cross_b[i, rows]
            mid = d1 * came + jnp.where(first, b, a)
            pass_z_b[i, rows] = d0 * mid + jnp.where(first, a, b)

            @pl.when(pair > 0)
            def _():
                bz_copy(i, j).start()

            pass_x_b[i, rows] = jnp.where(first, came, mid)
            bx_copy(i, j).start()
            used_b[i, rows] = jnp.where(first, mid, came)

    @pl.loop(0, groups + last + LAG)
    def _(t):
        step = t - (last - pair)
        active = jnp.logical_and(step >= 0, step < groups)
        late = step - LAG

        @pl.when(active)
        def _():
            for i in spread_of(0, step):
                chain_back(i)

        @pl.when(t < groups)
        def _():
            local_back(spread_of(mine, t) + spread_of(theirs, t))

        @pl.when(active)
        def _():
            finish_back(spread_of(mine, step), [used_b[i] for i in spread_of(0, step)])

        @pl.when(jnp.logical_and(late >= 0, late < groups))
        def _():
            for i in spread_of(0, late):
                for j in range(PARTS):
                    bx_copy(i, j).wait_recv()
            finish_back(spread_of(theirs, late), [part_b[i] for i in spread_of(0, late)])

    dec_copy.wait_send()
    for copy in sum_copies:
        copy.wait_send()

    @pl.loop(0, half)
    def _(i):
        for j in range(PARTS):
            s_copy(i, j).wait_send()
            x_copy(i, j).wait_send()
            bs_copy(i, j).wait_send()
            bx_copy(i, j).wait_send()

            @pl.when(pair < last)
            def _():
                z_copy(i, j).wait_send()

            @pl.when(pair > 0)
            def _():
                bz_copy(i, j).wait_send()


def deliver(*refs):
    sources, targets, sems = refs[:5], refs[5:10], refs[10]
    copies = [
        pltpu.make_async_copy(src, dst, sems.at[j]) for j, (src, dst) in enumerate(zip(sources, targets))
    ]
    for copy in copies:
        copy.start()
    for copy in copies:
        copy.wait()


def solution(mesh):
    n_seq, n_head = mesh.shape["seq"], mesh.shape["head"]

    def shards(queries, key_rows, value_rows, log_decay, gate_input, out_gain, prior_state, out_grad):
        length, features = queries.shape
        heads = log_decay.shape[1]
        half = heads // 2
        wide = (length, features)
        anywhere = pl.BlockSpec(memory_space=pl.ANY)
        vmem = pl.BlockSpec(memory_space=pltpu.VMEM)

        def states(count):
            return pltpu.VMEM((count, HD, HD), F32)

        dma = pltpu.SemaphoreType.DMA
        results = pl.pallas_call(
            functools.partial(kernel, n_seq, n_head, heads),
            out_shape=[pltpu.VMEM(wide, BF16)] * 5,
            in_specs=[anywhere, anywhere, anywhere, vmem, anywhere, vmem, anywhere, anywhere],
            out_specs=[vmem] * 5,
            scratch_shapes=[pltpu.VMEM(wide, BF16)] * 5
            + [states(heads)]
            + [
                pltpu.VMEM((heads, BLK, HD), F32),
                pltpu.VMEM((heads, BLK), F32),
                pltpu.VMEM((heads, HD), F32),
                pltpu.VMEM((heads, HD), F32),
            ]
            + [states(heads)] + [states(half)] * 5 + [states(heads)]
            + [states(heads)] + [states(half)] * 6
            + [
                pltpu.VMEM((heads, BLK, BLK), F32),
                pltpu.VMEM((heads, BLK, BLK), BF16),
                pltpu.VMEM((heads, BLK, HD), F32),
                pltpu.VMEM((heads, BLK, HD), F32),
                pltpu.VMEM((heads, BLK, HD), BF16),
                pltpu.VMEM((heads, BLK, HD), F32),
                pltpu.VMEM((heads, BLK, HD), F32),
                pltpu.VMEM((BLK, HD), F32),
                pltpu.VMEM((BLK, HD), F32),
                pltpu.VMEM((8, BLK), F32),
                pltpu.VMEM((n_head - 1, 8, BLK), F32),
                dma((6,)),
                dma,
                dma,
                dma((n_head - 1,)),
                dma((n_head - 1,)),
            ]
            + [dma((half * PARTS,))] * 12,
            compiler_params=pltpu.CompilerParams(
                collective_id=0, has_side_effects=True, vmem_limit_bytes=44 * 1024 * 1024
            ),
            cost_estimate=pl.CostEstimate(
                flops=4_000_000_000, bytes_accessed=12_000_000, transcendentals=2_000_000
            ),
        )(
            queries, key_rows, value_rows, log_decay.T, gate_input,
            out_gain.reshape(1, features), prior_state, out_grad,
        )
        return pl.pallas_call(
            deliver,
            out_shape=[jax.ShapeDtypeStruct(wide, BF16)] * 5,
            in_specs=[vmem] * 5,
            out_specs=[anywhere] * 5,
            scratch_shapes=[dma((5,))],
            cost_estimate=pl.CostEstimate(flops=0, bytes_accessed=10_000_000, transcendentals=0),
        )(*results)

    cut = P("seq", "head")
    return jax.shard_map(
        shards,
        mesh=mesh,
        in_specs=(cut, cut, cut, cut, cut, P("head"), P("head", None, None), cut),
        out_specs=(cut,) * 5,
        check_vma=False,
    )
```

```python
import functools

import jax
import jax.numpy as jnp
from jax import lax
from jax.experimental import pallas as pl
from jax.experimental.pallas import tpu as pltpu
from jax.sharding import PartitionSpec as P

BLK = 256
D = 8192
HD = 128
PARTS = 1
LAG = 2
HOP = 2
GROUP = 2
ROWS = HD // PARTS
epsilon = 1e-06
MESH = pl.DeviceIdType.MESH
F32 = jnp.float32
BF16 = jnp.bfloat16


def dot(a, b, ca, cb):
    return lax.dot_general(a, b, (((ca,), (cb,)), ((), ())), preferred_element_type=F32)


def kernel(
    n_seq, n_head, heads,
    q_hbm, k_hbm, v_hbm, ld_ref, gate_hbm, gain_ref, prior_hbm, og_hbm,
    att_hbm, gq_hbm, gk_hbm, gv_hbm, gg_hbm,
    q, k, v, gate, og, prior,
    att, gq, gk, gv, gg,
    run_col, run_row, dec, dec_x,
    own, cross, enter, part, pass_z, pass_x, used,
    own_b, cross_b, enter_b, part_b, pass_z_b, pass_x_b, used_b,
    wts, mix, ctx, gnorm, grad, gk_acc, gv_acc,
    sq_acc, rd_acc, sums, sums_in,
    in_sem, out_sem, dec_send, dec_recv, sum_send, sum_recv,
    s_send, s_recv, z_send, z_recv, x_send, x_recv,
    bs_send, bs_recv, bz_send, bz_recv, bx_send, bx_recv,
):
    half = heads // 2
    me = lax.axis_index("seq")
    row = lax.axis_index("head")
    pair, side = me // 2, me % 2
    last = n_seq // 2 - 1
    partner = me + 1 - 2 * side
    mine, theirs = side * half, (1 - side) * half

    barrier = pltpu.get_barrier_semaphore()

    def greet(**target):
        pl.semaphore_signal(barrier, inc=1, device_id=target, device_id_type=MESH)

    greet(seq=partner)
    for d in range(1, n_head):
        greet(head=lax.rem(row + d, n_head))

    @pl.when(pair > 0)
    def _():
        greet(seq=me - 2)

    @pl.when(pair < last)
    def _():
        greet(seq=me + 2)

    loads = [
        pltpu.make_async_copy(src, dst, in_sem.at[j])
        for j, (src, dst) in enumerate(
            [(k_hbm, k), (v_hbm, v), (q_hbm, q), (gate_hbm, gate), (og_hbm, og), (prior_hbm, prior)]
        )
    ]
    for load in loads:
        load.start()

    ti = lax.broadcasted_iota(jnp.int32, (BLK, BLK), 0)
    si = lax.broadcasted_iota(jnp.int32, (BLK, BLK), 1)
    causal = ti >= si
    low = jnp.where(causal, 1.0, 0.0).astype(F32)
    ld = ld_ref[...]
    col = lax.dot_general(
        low, ld, (((1,), (1,)), ((), ())), precision=lax.Precision.HIGHEST, preferred_element_type=F32
    )
    run_row[...] = lax.dot_general(
        ld, low, (((1,), (1,)), ((), ())), precision=lax.Precision.HIGHEST, preferred_element_type=F32
    )
    for h in range(heads):
        wide = jnp.broadcast_to(col[:, h : h + 1], (BLK, HD))
        run_col[h] = wide
        dec[h : h + 1, :] = jnp.exp(wide[BLK - 1 : BLK, :])

    def cols(h):
        return pl.ds(pl.multiple_of(h * HD, HD), HD)

    def send(src, dst, s, r, **target):
        return pltpu.make_async_remote_copy(
            src_ref=src, dst_ref=dst, send_sem=s, recv_sem=r, device_id=target, device_id_type=MESH
        )

    sum_copies = [
        send(sums, sums_in.at[d - 1], sum_send.at[d - 1], sum_recv.at[d - 1], head=lax.rem(row + d, n_head))
        for d in range(1, n_head)
    ]
    dec_copy = send(dec, dec_x, dec_send, dec_recv, seq=partner)

    def piece(ref, i, j):
        return ref.at[i, pl.ds(j * ROWS, ROWS)]

    def s_copy(i, j):
        n = i * PARTS + j
        return send(piece(own, theirs + i, j), piece(cross, i, j), s_send.at[n], s_recv.at[n], seq=partner)

    def z_copy(i, j):
        n = i * PARTS + j
        return send(piece(pass_z, i, j), piece(enter, i, j), z_send.at[n], z_recv.at[n], seq=me + 2)

    def x_copy(i, j):
        n = i * PARTS + j
        return send(piece(pass_x, i, j), piece(part, i, j), x_send.at[n], x_recv.at[n], seq=partner)

    def bs_copy(i, j):
        n = i * PARTS + j
        return send(piece(own_b, theirs + i, j), piece(cross_b, i, j), bs_send.at[n], bs_recv.at[n], seq=partner)

    def bz_copy(i, j):
        n = i * PARTS + j
        return send(piece(pass_z_b, i, j), piece(enter_b, i, j), bz_send.at[n], bz_recv.at[n], seq=me - 2)

    def bx_copy(i, j):
        n = i * PARTS + j
        return send(piece(pass_x_b, i, j), piece(part_b, i, j), bx_send.at[n], bx_recv.at[n], seq=partner)

    def remain_of(h):
        wide = run_col[h]
        return jnp.exp(wide[BLK - 1 : BLK, :] - wide)

    def summaries(hs):
        scaled = [(k[:, cols(h)].astype(F32) * remain_of(h)).astype(BF16) for h in hs]
        made = [dot(a, v[:, cols(h)], 0, 0) for a, h in zip(scaled, hs)]
        for h, state in zip(hs, made):
            own[h] = state

    loads[0].wait()
    loads[1].wait()
    pl.semaphore_wait(
        barrier, n_head + jnp.where(pair > 0, 1, 0) + jnp.where(pair < last, 1, 0)
    )
    dec_copy.start()

    def spread_of(start, g):
        return [start + g * GROUP + i for i in range(GROUP)]

    groups = half // GROUP

    @pl.loop(0, groups)
    def _(g):
        summaries(spread_of(theirs, g))
        for i in spread_of(0, g):
            for j in range(PARTS):
                s_copy(i, j).start()

    @pl.loop(0, groups)
    def _(g):
        summaries(spread_of(mine, g))

    for load in loads[2:]:
        load.wait()
    dec_copy.wait_recv()
    sq_acc[...] = jnp.zeros_like(sq_acc)
    rd_acc[...] = jnp.zeros_like(rd_acc)

    def within(hs):
        scores = [dot(q[:, cols(h)], k[:, cols(h)], 1, 1) for h in hs]
        ws = []
        for h in hs:
            wide = run_col[h]
            spread = jnp.concatenate([wide, wide], axis=1) - run_row[pl.ds(h, 1), :]
            ws.append(jnp.where(causal, jnp.exp(jnp.minimum(spread, 0.0)), 0.0))
        ms = [(a * w).astype(BF16) for a, w in zip(scores, ws)]
        rows = [dot(m, v[:, cols(h)], 1, 0) for m, h in zip(ms, hs)]
        opens = [jax.nn.sigmoid(gate[:, cols(h)].astype(F32)) for h in hs]
        norms = [og[:, cols(h)].astype(F32) * gain_ref[:, cols(h)] * o for h, o in zip(hs, opens)]
        for h, w, m, c, o in zip(hs, ws, ms, rows, norms):
            wts[h] = w
            mix[h] = m
            ctx[h] = c
            gnorm[h] = o

    def finish(hs):
        across = [dot(q[:, cols(h)], used[h].astype(BF16), 1, 0) for h in hs]
        cs = [ctx[h] + jnp.exp(run_col[h]) * a for h, a in zip(hs, across)]
        squares, dots = sq_acc[...], rd_acc[...]
        for h, c in zip(hs, cs):
            squares = squares + c * c
            dots = dots + c * gnorm[h]
        for h, c in zip(hs, cs):
            ctx[h] = c
        sq_acc[...] = squares
        rd_acc[...] = dots

    first = side == 0

    def chain(i):
        h = mine + i
        da, db = dec[pl.ds(h, 1), :], dec_x[pl.ds(h, 1), :]
        d0, d1 = jnp.where(first, da, db), jnp.where(first, db, da)
        for j in range(PARTS):
            rows = pl.ds(j * ROWS, ROWS)
            s_copy(i, j).wait_recv()

            @pl.when(pair == 0)
            def _():
                enter[i, rows] = prior[h, rows]

            @pl.when(pair > 0)
            def _():
                z_copy(i, j).wait_recv()

            came = enter[i, rows]
            a, b = own[h, rows], cross[i, rows]
            mid = d0 * came + jnp.where(first, a, b)
            pass_z[i, rows] = d1 * mid + jnp.where(first, b, a)

            @pl.when(pair < last)
            def _():
                z_copy(i, j).start()

            pass_x[i, rows] = jnp.where(first, mid, came)
            x_copy(i, j).start()
            used[h, rows] = jnp.where(first, came, mid)

    @pl.loop(0, half + max(half, HOP * last + LAG))
    def _(t):
        step = t - HOP * pair
        late = t - jnp.maximum(half, HOP * pair + LAG)

        @pl.when(jnp.logical_and(step >= 0, step < half))
        def _():
            chain(step)

        @pl.when(t < heads)
        def _():
            within([lax.rem(mine + t, heads)])

        @pl.when(jnp.logical_and(step >= 0, step < half))
        def _():
            finish([mine + step])

        @pl.when(jnp.logical_and(late >= 0, late < half))
        def _():
            for j in range(PARTS):
                x_copy(late, j).wait_recv()
            used[theirs + late] = part[late]
            finish([theirs + late])

    sums[...] = jnp.zeros_like(sums)
    sums[0:1, :] = jnp.sum(sq_acc[...].T, axis=0, keepdims=True)
    sums[1:2, :] = jnp.sum(rd_acc[...].T, axis=0, keepdims=True)
    for copy in sum_copies:
        copy.start()
    total = sums[...]
    for d, copy in enumerate(sum_copies):
        copy.wait_recv()
        total = total + sums_in[d]
    inv_row = lax.rsqrt(total[0:1, :] / D + epsilon)
    coef_row = inv_row * inv_row * inv_row * total[1:2, :] / D
    sq_acc[...] = jnp.broadcast_to(inv_row, (HD, BLK)).T
    rd_acc[...] = jnp.broadcast_to(coef_row, (HD, BLK)).T

    def gradients(hs):
        inv, coef = sq_acc[...], rd_acc[...]
        gs = [(inv * gnorm[h] - ctx[h] * coef).astype(BF16) for h in hs]
        scaled = [(q[:, cols(h)].astype(F32) * jnp.exp(run_col[h])).astype(BF16) for h in hs]
        made = [dot(a, g, 0, 0) for a, g in zip(scaled, gs)]
        for h, g, state in zip(hs, gs, made):
            grad[h] = g
            own_b[h] = state

    @pl.loop(0, groups)
    def _(g):
        gradients(spread_of(theirs, g))
        for i in spread_of(0, g):
            for j in range(PARTS):
                bs_copy(i, j).start()

    @pl.loop(0, groups)
    def _(g):
        gradients(spread_of(mine, g))

    def local_back(hs):
        gs = [grad[h] for h in hs]
        scores = [dot(g, v[:, cols(h)], 1, 1) for g, h in zip(gs, hs)]
        across = [dot(g, used[h].astype(BF16), 1, 1) for g, h in zip(gs, hs)]
        values = [dot(mix[h], g, 0, 0) for g, h in zip(gs, hs)]
        gms = [(a * wts[h]).astype(BF16) for a, h in zip(scores, hs)]
        queries = [dot(m, k[:, cols(h)], 1, 0) for m, h in zip(gms, hs)]
        keys = [dot(m, q[:, cols(h)], 0, 0) for m, h in zip(gms, hs)]
        queries = [
            (a + jnp.exp(run_col[h]) * b).astype(BF16) for a, b, h in zip(queries, across, hs)
        ]
        outs = []
        for h in hs:
            normed = ctx[h] * sq_acc[...]
            opened = jax.nn.sigmoid(gate[:, cols(h)].astype(F32))
            outs.append(
                (
                    (normed * gain_ref[:, cols(h)] * opened).astype(BF16),
                    (gnorm[h] * normed * (1.0 - opened)).astype(BF16),
                )
            )
        for h, a, b, c, (d, e) in zip(hs, queries, keys, values, outs):
            gq[:, cols(h)] = a
            gk_acc[h] = b
            gv_acc[h] = c
            att[:, cols(h)] = d
            gg[:, cols(h)] = e

    def finish_back(hs, states):
        states = [state.astype(BF16) for state in states]
        keys = [dot(v[:, cols(h)], a, 1, 1) for h, a in zip(hs, states)]
        values = [dot(k[:, cols(h)], a, 1, 0) for h, a in zip(hs, states)]
        done = []
        for h, a, b in zip(hs, keys, values):
            remain = remain_of(h)
            done.append(((gk_acc[h] + remain * a).astype(BF16), (gv_acc[h] + remain * b).astype(BF16)))
        for h, (a, b) in zip(hs, done):
            gk[:, cols(h)] = a
            gv[:, cols(h)] = b

    def chain_back(i):
        h = mine + i
        da, db = dec[pl.ds(h, 1), :], dec_x[pl.ds(h, 1), :]
        d0, d1 = jnp.where(first, da, db), jnp.where(first, db, da)
        for j in range(PARTS):
            rows = pl.ds(j * ROWS, ROWS)
            bs_copy(i, j).wait_recv()

            @pl.when(pair == last)
            def _():
                enter_b[i, rows] = jnp.zeros((ROWS, HD), F32)

            @pl.when(pair < last)
            def _():
                bz_copy(i, j).wait_recv()

            came = enter_b[i, rows]
            a, b = own_b[h, rows], cross_b[i, rows]
            mid = d1 * came + jnp.where(first, b, a)
            pass_z_b[i, rows] = d0 * mid + jnp.where(first, a, b)

            @pl.when(pair > 0)
            def _():
                bz_copy(i, j).start()

            pass_x_b[i, rows] = jnp.where(first, came, mid)
            bx_copy(i, j).start()
            used_b[i, rows] = jnp.where(first, mid, came)

    def stores(kind, h):
        pairs = [(att, att_hbm), (gq, gq_hbm), (gg, gg_hbm), (gk, gk_hbm), (gv, gv_hbm)]
        return [
            pltpu.make_async_copy(pairs[j][0].at[:, cols(h)], pairs[j][1].at[:, cols(h)], out_sem.at[j, h])
            for j in ((0, 1, 2), (3, 4), (0, 1, 2, 3, 4))[kind]
        ]

    @pl.loop(0, half + max(half, HOP * last + LAG))
    def _(t):
        step = t - HOP * (last - pair)
        late = t - jnp.maximum(half, HOP * (last - pair) + LAG)

        @pl.when(jnp.logical_and(step >= 0, step < half))
        def _():
            chain_back(step)

        @pl.when(t < heads)
        def _():
            h = lax.rem(mine + t, heads)
            local_back([h])
            for store in stores(0, h):
                store.start()

        @pl.when(jnp.logical_and(step >= 0, step < half))
        def _():
            finish_back([mine + step], [used_b[step]])
            for store in stores(1, mine + step):
                store.start()

        @pl.when(jnp.logical_and(late >= 0, late < half))
        def _():
            for j in range(PARTS):
                bx_copy(late, j).wait_recv()
            finish_back([theirs + late], [part_b[late]])
            for store in stores(1, theirs + late):
                store.start()

    dec_copy.wait_send()
    for copy in sum_copies:
        copy.wait_send()

    @pl.loop(0, heads)
    def _(h):
        for store in stores(2, h):
            store.wait()

    @pl.loop(0, half)
    def _(i):
        for j in range(PARTS):
            s_copy(i, j).wait_send()
            x_copy(i, j).wait_send()
            bs_copy(i, j).wait_send()
            bx_copy(i, j).wait_send()

            @pl.when(pair < last)
            def _():
                z_copy(i, j).wait_send()

            @pl.when(pair > 0)
            def _():
                bz_copy(i, j).wait_send()


def deliver(rows, *refs):
    sources, targets, staged, (in_sem, out_sem) = refs[:5], refs[5:10], refs[10:15], refs[15:]
    loads, stores = [], []
    for j in range(10):
        part = pl.ds(j // 5 * rows, rows)
        a, b, c = sources[j % 5].at[part], staged[j % 5].at[part], targets[j % 5].at[part]
        loads.append(pltpu.make_async_copy(a, b, in_sem.at[j]))
        stores.append(pltpu.make_async_copy(b, c, out_sem.at[j]))
    for load in loads:
        load.start()
    for load, store in zip(loads, stores):
        load.wait()
        store.start()
    for store in stores:
        store.wait()


def solution(mesh):
    n_seq, n_head = mesh.shape["seq"], mesh.shape["head"]

    def shards(queries, key_rows, value_rows, log_decay, gate_input, out_gain, prior_state, out_grad):
        length, features = queries.shape
        heads = log_decay.shape[1]
        half = heads // 2
        wide = (length, features)
        anywhere = pl.BlockSpec(memory_space=pl.ANY)
        vmem = pl.BlockSpec(memory_space=pltpu.VMEM)

        def states(count):
            return pltpu.VMEM((count, HD, HD), F32)

        dma = pltpu.SemaphoreType.DMA
        results = pl.pallas_call(
            functools.partial(kernel, n_seq, n_head, heads),
            out_shape=[jax.ShapeDtypeStruct(wide, BF16)] * 5,
            in_specs=[anywhere, anywhere, anywhere, vmem, anywhere, vmem, anywhere, anywhere],
            out_specs=[anywhere] * 5,
            scratch_shapes=[pltpu.VMEM(wide, BF16)] * 5
            + [states(heads)]
            + [pltpu.VMEM(wide, BF16)] * 5
            + [
                pltpu.VMEM((heads, BLK, HD), F32),
                pltpu.VMEM((heads, BLK), F32),
                pltpu.VMEM((heads, HD), F32),
                pltpu.VMEM((heads, HD), F32),
            ]
            + [states(heads)] + [states(half)] * 5 + [states(heads)]
            + [states(heads)] + [states(half)] * 6
            + [
                pltpu.VMEM((heads, BLK, BLK), F32),
                pltpu.VMEM((heads, BLK, BLK), BF16),
                pltpu.VMEM((heads, BLK, HD), F32),
                pltpu.VMEM((heads, BLK, HD), F32),
                pltpu.VMEM((heads, BLK, HD), BF16),
                pltpu.VMEM((heads, BLK, HD), F32),
                pltpu.VMEM((heads, BLK, HD), F32),
                pltpu.VMEM((BLK, HD), F32),
                pltpu.VMEM((BLK, HD), F32),
                pltpu.VMEM((8, BLK), F32),
                pltpu.VMEM((n_head - 1, 8, BLK), F32),
                dma((6,)),
                dma((5, heads)),
                dma,
                dma,
                dma((n_head - 1,)),
                dma((n_head - 1,)),
            ]
            + [dma((half * PARTS,))] * 12,
            compiler_params=pltpu.CompilerParams(
                collective_id=0, has_side_effects=True, vmem_limit_bytes=60 * 1024 * 1024
            ),
            cost_estimate=pl.CostEstimate(
                flops=4_000_000_000, bytes_accessed=12_000_000, transcendentals=2_000_000
            ),
        )(
            queries, key_rows, value_rows, log_decay.T, gate_input,
            out_gain.reshape(1, features), prior_state, out_grad,
        )
        return pl.pallas_call(
            functools.partial(deliver, length // 2),
            out_shape=[jax.ShapeDtypeStruct(wide, BF16)] * 5,
            in_specs=[anywhere] * 5,
            out_specs=[anywhere] * 5,
            scratch_shapes=[pltpu.VMEM(wide, BF16)] * 5 + [dma((10,)), dma((10,))],
            compiler_params=pltpu.CompilerParams(vmem_limit_bytes=60 * 1024 * 1024),
            cost_estimate=pl.CostEstimate(flops=0, bytes_accessed=10_000_000, transcendentals=0),
        )(*results)

    cut = P("seq", "head")
    return jax.shard_map(
        shards,
        mesh=mesh,
        in_specs=(cut, cut, cut, cut, cut, P("head"), P("head", None, None), cut),
        out_specs=(cut,) * 5,
        check_vma=False,
    )
```

```python
import functools

import jax
import jax.numpy as jnp
from jax import lax
from jax.experimental import pallas as pl
from jax.experimental.pallas import tpu as pltpu
from jax.sharding import PartitionSpec as P

BLK = 256
D = 8192
HD = 128
PARTS = 1
LAG = 2
HOP = 2
GROUP = 2
ROWS = HD // PARTS
epsilon = 1e-06
MESH = pl.DeviceIdType.MESH
F32 = jnp.float32
BF16 = jnp.bfloat16


def dot(a, b, ca, cb):
    return lax.dot_general(a, b, (((ca,), (cb,)), ((), ())), preferred_element_type=F32)


def kernel(
    n_seq, n_head, heads,
    q_hbm, k_hbm, v_hbm, ld_ref, gate_hbm, gain_ref, prior_hbm, og_hbm,
    att_hbm, gq_hbm, gk_hbm, gv_hbm, gg_hbm,
    q, k, v, gate, og, prior,
    att, gq, gk, gv, gg,
    run_col, run_row, dec, dec_x,
    own, cross, enter, part, pass_z, pass_x, used,
    own_b, cross_b, enter_b, part_b, pass_z_b, pass_x_b, used_b,
    wts, mix, ctx, gnorm, grad, gk_acc, gv_acc,
    sq_acc, rd_acc, sums, sums_in,
    in_sem, out_sem, dec_send, dec_recv, sum_send, sum_recv,
    s_send, s_recv, z_send, z_recv, x_send, x_recv,
    bs_send, bs_recv, bz_send, bz_recv, bx_send, bx_recv,
):
    half = heads // 2
    me = lax.axis_index("seq")
    row = lax.axis_index("head")
    pair, side = me // 2, me % 2
    last = n_seq // 2 - 1
    partner = me + 1 - 2 * side
    mine, theirs = side * half, (1 - side) * half

    barrier = pltpu.get_barrier_semaphore()

    def greet(**target):
        pl.semaphore_signal(barrier, inc=1, device_id=target, device_id_type=MESH)

    greet(seq=partner)
    for d in range(1, n_head):
        greet(head=lax.rem(row + d, n_head))

    @pl.when(pair > 0)
    def _():
        greet(seq=me - 2)

    @pl.when(pair < last)
    def _():
        greet(seq=me + 2)

    loads = [
        pltpu.make_async_copy(src, dst, in_sem.at[j])
        for j, (src, dst) in enumerate(
            [(k_hbm, k), (v_hbm, v), (q_hbm, q), (gate_hbm, gate), (og_hbm, og), (prior_hbm, prior)]
        )
    ]
    for load in loads:
        load.start()

    ti = lax.broadcasted_iota(jnp.int32, (BLK, BLK), 0)
    si = lax.broadcasted_iota(jnp.int32, (BLK, BLK), 1)
    causal = ti >= si
    low = jnp.where(causal, 1.0, 0.0).astype(F32)
    ld = ld_ref[...]
    col = lax.dot_general(
        low, ld, (((1,), (1,)), ((), ())), precision=lax.Precision.HIGHEST, preferred_element_type=F32
    )
    run_row[...] = lax.dot_general(
        ld, low, (((1,), (1,)), ((), ())), precision=lax.Precision.HIGHEST, preferred_element_type=F32
    )
    for h in range(heads):
        wide = jnp.broadcast_to(col[:, h : h + 1], (BLK, HD))
        run_col[h] = wide
        dec[h : h + 1, :] = jnp.exp(wide[BLK - 1 : BLK, :])

    def cols(h):
        return pl.ds(pl.multiple_of(h * HD, HD), HD)

    def send(src, dst, s, r, **target):
        return pltpu.make_async_remote_copy(
            src_ref=src, dst_ref=dst, send_sem=s, recv_sem=r, device_id=target, device_id_type=MESH
        )

    sum_copies = [
        send(sums, sums_in.at[d - 1], sum_send.at[d - 1], sum_recv.at[d - 1], head=lax.rem(row + d, n_head))
        for d in range(1, n_head)
    ]
    dec_copy = send(dec, dec_x, dec_send, dec_recv, seq=partner)

    def piece(ref, i, j):
        return ref.at[i, pl.ds(j * ROWS, ROWS)]

    def s_copy(i, j):
        n = i * PARTS + j
        return send(piece(own, theirs + i, j), piece(cross, i, j), s_send.at[n], s_recv.at[n], seq=partner)

    def z_copy(i, j):
        n = i * PARTS + j
        return send(piece(pass_z, i, j), piece(enter, i, j), z_send.at[n], z_recv.at[n], seq=me + 2)

    def x_copy(i, j):
        n = i * PARTS + j
        return send(piece(pass_x, i, j), piece(part, i, j), x_send.at[n], x_recv.at[n], seq=partner)

    def bs_copy(i, j):
        n = i * PARTS + j
        return send(piece(own_b, theirs + i, j), piece(cross_b, i, j), bs_send.at[n], bs_recv.at[n], seq=partner)

    def bz_copy(i, j):
        n = i * PARTS + j
        return send(piece(pass_z_b, i, j), piece(enter_b, i, j), bz_send.at[n], bz_recv.at[n], seq=me - 2)

    def bx_copy(i, j):
        n = i * PARTS + j
        return send(piece(pass_x_b, i, j), piece(part_b, i, j), bx_send.at[n], bx_recv.at[n], seq=partner)

    def remain_of(h):
        wide = run_col[h]
        return jnp.exp(wide[BLK - 1 : BLK, :] - wide)

    def summaries(hs):
        scaled = [(k[:, cols(h)].astype(F32) * remain_of(h)).astype(BF16) for h in hs]
        made = [dot(a, v[:, cols(h)], 0, 0) for a, h in zip(scaled, hs)]
        for h, state in zip(hs, made):
            own[h] = state

    loads[0].wait()
    loads[1].wait()
    pl.semaphore_wait(
        barrier, n_head + jnp.where(pair > 0, 1, 0) + jnp.where(pair < last, 1, 0)
    )
    dec_copy.start()

    def spread_of(start, g):
        return [start + g * GROUP + i for i in range(GROUP)]

    groups = half // GROUP

    @pl.loop(0, groups)
    def _(g):
        summaries(spread_of(theirs, g))
        for i in spread_of(0, g):
            for j in range(PARTS):
                s_copy(i, j).start()

    @pl.loop(0, groups)
    def _(g):
        summaries(spread_of(mine, g))

    for load in loads[2:]:
        load.wait()
    dec_copy.wait_recv()
    sq_acc[...] = jnp.zeros_like(sq_acc)
    rd_acc[...] = jnp.zeros_like(rd_acc)

    def within(hs):
        scores = [dot(q[:, cols(h)], k[:, cols(h)], 1, 1) for h in hs]
        ws = []
        for h in hs:
            wide = run_col[h]
            spread = jnp.concatenate([wide, wide], axis=1) - run_row[pl.ds(h, 1), :]
            ws.append(jnp.where(causal, jnp.exp(jnp.minimum(spread, 0.0)), 0.0))
        ms = [(a * w).astype(BF16) for a, w in zip(scores, ws)]
        rows = [dot(m, v[:, cols(h)], 1, 0) for m, h in zip(ms, hs)]
        opens = [jax.nn.sigmoid(gate[:, cols(h)].astype(F32)) for h in hs]
        norms = [og[:, cols(h)].astype(F32) * gain_ref[:, cols(h)] * o for h, o in zip(hs, opens)]
        for h, w, m, c, o in zip(hs, ws, ms, rows, norms):
            wts[h] = w
            mix[h] = m
            ctx[h] = c
            gnorm[h] = o

    def finish(hs):
        across = [dot(q[:, cols(h)], used[h].astype(BF16), 1, 0) for h in hs]
        cs = [ctx[h] + jnp.exp(run_col[h]) * a for h, a in zip(hs, across)]
        squares, dots = sq_acc[...], rd_acc[...]
        for h, c in zip(hs, cs):
            squares = squares + c * c
            dots = dots + c * gnorm[h]
        for h, c in zip(hs, cs):
            ctx[h] = c
        sq_acc[...] = squares
        rd_acc[...] = dots

    first = side == 0

    def chain(i):
        h = mine + i
        da, db = dec[pl.ds(h, 1), :], dec_x[pl.ds(h, 1), :]
        d0, d1 = jnp.where(first, da, db), jnp.where(first, db, da)
        for j in range(PARTS):
            rows = pl.ds(j * ROWS, ROWS)
            s_copy(i, j).wait_recv()

            @pl.when(pair == 0)
            def _():
                enter[i, rows] = prior[h, rows]

            @pl.when(pair > 0)
            def _():
                z_copy(i, j).wait_recv()

            came = enter[i, rows]
            a, b = own[h, rows], cross[i, rows]
            mid = d0 * came + jnp.where(first, a, b)
            pass_z[i, rows] = d1 * mid + jnp.where(first, b, a)

            @pl.when(pair < last)
            def _():
                z_copy(i, j).start()

            pass_x[i, rows] = jnp.where(first, mid, came)
            x_copy(i, j).start()
            used[h, rows] = jnp.where(first, came, mid)

    @pl.loop(0, half + max(half, HOP * last + LAG))
    def _(t):
        step = t - HOP * pair
        late = t - jnp.maximum(half, HOP * pair + LAG)

        @pl.when(jnp.logical_and(step >= 0, step < half))
        def _():
            chain(step)

        def closes(n):
            return (n >= 0) & (n < half) & (lax.rem(n + GROUP, GROUP) == GROUP - 1)

        @pl.when((t < heads) & (lax.rem(t, GROUP) == 0))
        def _():
            h = lax.rem(mine + t, heads)
            within([h + i for i in range(GROUP)])

        @pl.when(closes(step))
        def _():
            finish([mine + step - i for i in range(GROUP)])

        @pl.when(closes(late))
        def _():
            for i in range(GROUP):
                for j in range(PARTS):
                    x_copy(late - i, j).wait_recv()
                used[theirs + late - i] = part[late - i]
            finish([theirs + late - i for i in range(GROUP)])

    sums[...] = jnp.zeros_like(sums)
    sums[0:1, :] = jnp.sum(sq_acc[...].T, axis=0, keepdims=True)
    sums[1:2, :] = jnp.sum(rd_acc[...].T, axis=0, keepdims=True)
    for copy in sum_copies:
        copy.start()
    total = sums[...]
    for d, copy in enumerate(sum_copies):
        copy.wait_recv()
        total = total + sums_in[d]
    inv_row = lax.rsqrt(total[0:1, :] / D + epsilon)
    coef_row = inv_row * inv_row * inv_row * total[1:2, :] / D
    sq_acc[...] = jnp.broadcast_to(inv_row, (HD, BLK)).T
    rd_acc[...] = jnp.broadcast_to(coef_row, (HD, BLK)).T

    def gradients(hs):
        inv, coef = sq_acc[...], rd_acc[...]
        gs = [(inv * gnorm[h] - ctx[h] * coef).astype(BF16) for h in hs]
        scaled = [(q[:, cols(h)].astype(F32) * jnp.exp(run_col[h])).astype(BF16) for h in hs]
        made = [dot(a, g, 0, 0) for a, g in zip(scaled, gs)]
        for h, g, state in zip(hs, gs, made):
            grad[h] = g
            own_b[h] = state

    @pl.loop(0, groups)
    def _(g):
        gradients(spread_of(theirs, g))
        for i in spread_of(0, g):
            for j in range(PARTS):
                bs_copy(i, j).start()

    @pl.loop(0, groups)
    def _(g):
        gradients(spread_of(mine, g))

    def local_back(hs):
        gs = [grad[h] for h in hs]
        scores = [dot(g, v[:, cols(h)], 1, 1) for g, h in zip(gs, hs)]
        across = [dot(g, used[h].astype(BF16), 1, 1) for g, h in zip(gs, hs)]
        values = [dot(mix[h], g, 0, 0) for g, h in zip(gs, hs)]
        gms = [(a * wts[h]).astype(BF16) for a, h in zip(scores, hs)]
        queries = [dot(m, k[:, cols(h)], 1, 0) for m, h in zip(gms, hs)]
        keys = [dot(m, q[:, cols(h)], 0, 0) for m, h in zip(gms, hs)]
        queries = [
            (a + jnp.exp(run_col[h]) * b).astype(BF16) for a, b, h in zip(queries, across, hs)
        ]
        outs = []
        for h in hs:
            normed = ctx[h] * sq_acc[...]
            opened = jax.nn.sigmoid(gate[:, cols(h)].astype(F32))
            outs.append(
                (
                    (normed * gain_ref[:, cols(h)] * opened).astype(BF16),
                    (gnorm[h] * normed * (1.0 - opened)).astype(BF16),
                )
            )
        for h, a, b, c, (d, e) in zip(hs, queries, keys, values, outs):
            gq[:, cols(h)] = a
            gk_acc[h] = b
            gv_acc[h] = c
            att[:, cols(h)] = d
            gg[:, cols(h)] = e

    def finish_back(hs, states):
        states = [state.astype(BF16) for state in states]
        keys = [dot(v[:, cols(h)], a, 1, 1) for h, a in zip(hs, states)]
        values = [dot(k[:, cols(h)], a, 1, 0) for h, a in zip(hs, states)]
        done = []
        for h, a, b in zip(hs, keys, values):
            remain = remain_of(h)
            done.append(((gk_acc[h] + remain * a).astype(BF16), (gv_acc[h] + remain * b).astype(BF16)))
        for h, (a, b) in zip(hs, done):
            gk[:, cols(h)] = a
            gv[:, cols(h)] = b

    def chain_back(i):
        h = mine + i
        da, db = dec[pl.ds(h, 1), :], dec_x[pl.ds(h, 1), :]
        d0, d1 = jnp.where(first, da, db), jnp.where(first, db, da)
        for j in range(PARTS):
            rows = pl.ds(j * ROWS, ROWS)
            bs_copy(i, j).wait_recv()

            @pl.when(pair == last)
            def _():
                enter_b[i, rows] = jnp.zeros((ROWS, HD), F32)

            @pl.when(pair < last)
            def _():
                bz_copy(i, j).wait_recv()

            came = enter_b[i, rows]
            a, b = own_b[h, rows], cross_b[i, rows]
            mid = d1 * came + jnp.where(first, b, a)
            pass_z_b[i, rows] = d0 * mid + jnp.where(first, a, b)

            @pl.when(pair > 0)
            def _():
                bz_copy(i, j).start()

            pass_x_b[i, rows] = jnp.where(first, came, mid)
            bx_copy(i, j).start()
            used_b[i, rows] = jnp.where(first, mid, came)

    def stores(kind, h):
        pairs = [(att, att_hbm), (gq, gq_hbm), (gg, gg_hbm), (gk, gk_hbm), (gv, gv_hbm)]
        return [
            pltpu.make_async_copy(pairs[j][0].at[:, cols(h)], pairs[j][1].at[:, cols(h)], out_sem.at[j, h])
            for j in ((0, 1, 2), (3, 4), (0, 1, 2, 3, 4))[kind]
        ]

    @pl.loop(0, half + max(half, HOP * last + LAG))
    def _(t):
        step = t - HOP * (last - pair)
        late = t - jnp.maximum(half, HOP * (last - pair) + LAG)

        @pl.when(jnp.logical_and(step >= 0, step < half))
        def _():
            chain_back(step)

        def closes(n):
            return (n >= 0) & (n < half) & (lax.rem(n + GROUP, GROUP) == GROUP - 1)

        @pl.when((t < heads) & (lax.rem(t, GROUP) == 0))
        def _():
            hs = [lax.rem(mine + t, heads) + i for i in range(GROUP)]
            local_back(hs)
            for h in hs:
                for store in stores(0, h):
                    store.start()

        @pl.when(closes(step))
        def _():
            hs = [step - i for i in range(GROUP)]
            finish_back([mine + i for i in hs], [used_b[i] for i in hs])
            for i in hs:
                for store in stores(1, mine + i):
                    store.start()

        @pl.when(closes(late))
        def _():
            hs = [late - i for i in range(GROUP)]
            for i in hs:
                for j in range(PARTS):
                    bx_copy(i, j).wait_recv()
            finish_back([theirs + i for i in hs], [part_b[i] for i in hs])
            for i in hs:
                for store in stores(1, theirs + i):
                    store.start()

    dec_copy.wait_send()
    for copy in sum_copies:
        copy.wait_send()

    @pl.loop(0, heads)
    def _(h):
        for store in stores(2, h):
            store.wait()

    @pl.loop(0, half)
    def _(i):
        for j in range(PARTS):
            s_copy(i, j).wait_send()
            x_copy(i, j).wait_send()
            bs_copy(i, j).wait_send()
            bx_copy(i, j).wait_send()

            @pl.when(pair < last)
            def _():
                z_copy(i, j).wait_send()

            @pl.when(pair > 0)
            def _():
                bz_copy(i, j).wait_send()


def deliver(rows, *refs):
    sources, targets, staged, (in_sem, out_sem) = refs[:5], refs[5:10], refs[10:15], refs[15:]
    loads, stores = [], []
    for j in range(10):
        part = pl.ds(j // 5 * rows, rows)
        a, b, c = sources[j % 5].at[part], staged[j % 5].at[part], targets[j % 5].at[part]
        loads.append(pltpu.make_async_copy(a, b, in_sem.at[j]))
        stores.append(pltpu.make_async_copy(b, c, out_sem.at[j]))
    for load in loads:
        load.start()
    for load, store in zip(loads, stores):
        load.wait()
        store.start()
    for store in stores:
        store.wait()


def solution(mesh):
    n_seq, n_head = mesh.shape["seq"], mesh.shape["head"]

    def shards(queries, key_rows, value_rows, log_decay, gate_input, out_gain, prior_state, out_grad):
        length, features = queries.shape
        heads = log_decay.shape[1]
        half = heads // 2
        wide = (length, features)
        anywhere = pl.BlockSpec(memory_space=pl.ANY)
        vmem = pl.BlockSpec(memory_space=pltpu.VMEM)

        def states(count):
            return pltpu.VMEM((count, HD, HD), F32)

        dma = pltpu.SemaphoreType.DMA
        results = pl.pallas_call(
            functools.partial(kernel, n_seq, n_head, heads),
            out_shape=[jax.ShapeDtypeStruct(wide, BF16)] * 5,
            in_specs=[anywhere, anywhere, anywhere, vmem, anywhere, vmem, anywhere, anywhere],
            out_specs=[anywhere] * 5,
            scratch_shapes=[pltpu.VMEM(wide, BF16)] * 5
            + [states(heads)]
            + [pltpu.VMEM(wide, BF16)] * 5
            + [
                pltpu.VMEM((heads, BLK, HD), F32),
                pltpu.VMEM((heads, BLK), F32),
                pltpu.VMEM((heads, HD), F32),
                pltpu.VMEM((heads, HD), F32),
            ]
            + [states(heads)] + [states(half)] * 5 + [states(heads)]
            + [states(heads)] + [states(half)] * 6
            + [
                pltpu.VMEM((heads, BLK, BLK), F32),
                pltpu.VMEM((heads, BLK, BLK), BF16),
                pltpu.VMEM((heads, BLK, HD), F32),
                pltpu.VMEM((heads, BLK, HD), F32),
                pltpu.VMEM((heads, BLK, HD), BF16),
                pltpu.VMEM((heads, BLK, HD), F32),
                pltpu.VMEM((heads, BLK, HD), F32),
                pltpu.VMEM((BLK, HD), F32),
                pltpu.VMEM((BLK, HD), F32),
                pltpu.VMEM((8, BLK), F32),
                pltpu.VMEM((n_head - 1, 8, BLK), F32),
                dma((6,)),
                dma((5, heads)),
                dma,
                dma,
                dma((n_head - 1,)),
                dma((n_head - 1,)),
            ]
            + [dma((half * PARTS,))] * 12,
            compiler_params=pltpu.CompilerParams(
                collective_id=0, has_side_effects=True, vmem_limit_bytes=60 * 1024 * 1024
            ),
            cost_estimate=pl.CostEstimate(
                flops=4_000_000_000, bytes_accessed=12_000_000, transcendentals=2_000_000
            ),
        )(
            queries, key_rows, value_rows, log_decay.T, gate_input,
            out_gain.reshape(1, features), prior_state, out_grad,
        )
        return pl.pallas_call(
            functools.partial(deliver, length // 2),
            out_shape=[jax.ShapeDtypeStruct(wide, BF16)] * 5,
            in_specs=[anywhere] * 5,
            out_specs=[anywhere] * 5,
            scratch_shapes=[pltpu.VMEM(wide, BF16)] * 5 + [dma((10,)), dma((10,))],
            compiler_params=pltpu.CompilerParams(vmem_limit_bytes=60 * 1024 * 1024),
            cost_estimate=pl.CostEstimate(flops=0, bytes_accessed=10_000_000, transcendentals=0),
        )(*results)

    cut = P("seq", "head")
    return jax.shard_map(
        shards,
        mesh=mesh,
        in_specs=(cut, cut, cut, cut, cut, P("head"), P("head", None, None), cut),
        out_specs=(cut,) * 5,
        check_vma=False,
    )
```
